32 devices in a mesh: groups: 2 (over x), long: 16 (over z, y, core).
Axes of the slice: x: 2, y: 2, z: 4, core: 2. Of those that a mesh axis runs over, the one named last changes fastest.
Arguments:
- initial_state: float32 [2, 8192, 128], P(None, ('groups', 'long')), parts along dimension 1, may hold values from -6 to 6
- adjoint_state: float32 [2, 8192, 128], P(None, ('groups', 'long')), parts along dimension 1, may hold values from -6 to 6
- current_gates: float32 [8, 2, 128, 128], P('groups'), parts along dimension 0, may hold values from -0.375 to 0.375
Outputs:
- final_state: float32 [2, 8192, 128], P(None, ('groups', 'long')), parts along dimension 1
- final_adjoint: float32 [2, 8192, 128], P(None, ('groups', 'long')), parts along dimension 1
The draws below stay inside these ranges and needn't reach their ends.
There are 2 independent parts, one for each index of `groups`. The reference program is written for one: setup_inputs(seed, part) draws one part's arguments, and reference() takes and returns one part's arrays. A program takes and returns all parts, laid end to end along the dimension named above; each array names one. Nothing has to cross between parts.
All inputs are finite; a program needn't handle non-finite values.
Results may differ from the reference program's by a relative error of at most 0.00017.
Values sent between devices are 32-bit elements; how exact they have to be, the bound alone decides.
No kernel may reach another device: no remote copies, remote signals or barrier semaphores. Data moves between devices by JAX's collectives and lax.ppermute only.
A program may use at most 64 MiB of HBM per device.

```python
import jax
import jax.numpy as jnp
from jax import lax

GATE = 128
SECTIONS = 4
NS_ITERS = 8
AMP_ROWS = 4096
N_LONG = 16


def level_of(own_key, extent, pieces, least, high):
    loudness, own = 1.0, jax.random.fold_in(own_key, 6)
    for position, blocks in pieces:
        draws = jnp.exp(jax.random.uniform(jax.random.fold_in(own, position), (blocks,), jnp.float32, least / len(pieces), high / len(pieces)))
        loudness = loudness * jnp.repeat(draws, extent[position] // blocks).reshape([-1 if axis == position else 1 for axis in range(len(extent))])
    return loudness


def bell_draw(key, shape, spread, bound, pieces=(), dtype=jnp.bfloat16):
    values = spread * jax.random.normal(key, shape, jnp.float32)
    if pieces:
        values = values * level_of(key, shape, pieces, -0.22, 0.18)
    return jnp.clip(values, -bound, bound).astype(dtype)


def setup_inputs(seed: int = 0, part: int = 0) -> dict:
    seeds = jax.random.split(jax.random.key(seed), 4)
    part_keys = jax.random.split(jax.random.fold_in(seeds[3], part), 4)
    initial_state = bell_draw(part_keys[0], (2, AMP_ROWS, GATE), 1.0, 6.0, ((1, 16),), jnp.float32)
    adjoint_state = bell_draw(part_keys[1], (2, AMP_ROWS, GATE), 1.0, 6.0, ((1, 16),), jnp.float32)
    current_gates = bell_draw(part_keys[2], (SECTIONS, 2, GATE, GATE), (2 * GATE) ** -0.5, 0.375, (), jnp.float32)
    return {"initial_state": initial_state, "adjoint_state": adjoint_state, "current_gates": current_gates}


HIGHEST = lax.Precision.HIGHEST

def einsum_high(pattern, left_side, right_side):
    return jnp.einsum(pattern, left_side, right_side, precision=HIGHEST, preferred_element_type=jnp.float32)

def matmul_high(left_side, right_side):
    return jnp.dot(left_side, right_side, precision=HIGHEST, preferred_element_type=jnp.float32)

def rows_product(left_side, right_side):
    return lax.dot_general(left_side, right_side, (((0,), (0,)), ((), ())), precision=HIGHEST, preferred_element_type=jnp.float32)

def polar_factor(summed_real, summed_imag, sweeps):
    norm_scale = lax.rsqrt(jnp.sum(summed_real * summed_real + summed_imag * summed_imag) + 1e-06)
    iterate_real = summed_real * norm_scale
    iterate_imag = summed_imag * norm_scale
    for sweep_index in range(sweeps):
        gram_real = rows_product(iterate_real, iterate_real) + rows_product(iterate_imag, iterate_imag)
        gram_imag = rows_product(iterate_real, iterate_imag) - rows_product(iterate_imag, iterate_real)
        product_real = matmul_high(iterate_real, gram_real) - matmul_high(iterate_imag, gram_imag)
        product_imag = matmul_high(iterate_real, gram_imag) + matmul_high(iterate_imag, gram_real)
        iterate_real = 1.5 * iterate_real - 0.5 * product_real
        iterate_imag = 1.5 * iterate_imag - 0.5 * product_imag
    return (iterate_real, iterate_imag)

def split_view(amplitudes, partner_bit):
    outer_count = N_LONG // 2 ** (partner_bit + 1)
    inner_count = amplitudes.shape[1] // (2 * outer_count)
    lane_half = amplitudes.shape[2] // 2
    return amplitudes.reshape(amplitudes.shape[0], outer_count, 2, inner_count, 2, lane_half)

def apply_gate(gate_real, gate_imag, viewed):
    lane_half = gate_real.shape[0] // 2
    blocks_real = gate_real.reshape(2, lane_half, 2, lane_half)
    blocks_imag = gate_imag.reshape(2, lane_half, 2, lane_half)
    pattern = 'acbd,hbmed->hamec'
    out_real = einsum_high(pattern, blocks_real, viewed[0]) - einsum_high(pattern, blocks_imag, viewed[1])
    out_imag = einsum_high(pattern, blocks_real, viewed[1]) + einsum_high(pattern, blocks_imag, viewed[0])
    return jnp.stack([out_real, out_imag])

def environment(adjoint_view, state_view):
    pattern = 'hamec,hbmed->acbd'
    summed_real = einsum_high(pattern, adjoint_view[0], state_view[0]) + einsum_high(pattern, adjoint_view[1], state_view[1])
    summed_imag = einsum_high(pattern, adjoint_view[1], state_view[0]) - einsum_high(pattern, adjoint_view[0], state_view[1])
    gate_width = summed_real.shape[0] * summed_real.shape[1]
    return (summed_real.reshape(gate_width, gate_width), summed_imag.reshape(gate_width, gate_width))

def reference(initial_state, adjoint_state, current_gates):
    bit_count = N_LONG.bit_length() - 1
    partner_bits = [bit_count - 1, bit_count // 2, 0, 1]
    state_now = initial_state
    adjoint_now = adjoint_state
    for section_index in range(SECTIONS):
        partner_bit = partner_bits[section_index % 4]
        state_view = split_view(state_now, partner_bit)
        adjoint_view = apply_gate(current_gates[section_index, 0], current_gates[section_index, 1], split_view(adjoint_now, partner_bit))
        summed_real, summed_imag = environment(adjoint_view, state_view)
        gate_real, gate_imag = polar_factor(summed_real, summed_imag, NS_ITERS)
        state_view = apply_gate(gate_real, gate_imag, state_view)
        state_now = state_view.reshape(initial_state.shape)
        adjoint_now = adjoint_view.reshape(adjoint_state.shape)
    return (state_now, adjoint_now)
```

```python
import functools

import jax
import jax.numpy as jnp
import numpy as np
from jax import lax
from jax.experimental import pallas as pl
from jax.experimental.pallas import tpu as pltpu
from jax.sharding import PartitionSpec as P

SECTIONS = 4
NS_ITERS = 8

F32, BF16 = jnp.float32, jnp.bfloat16
NN = (((1,), (0,)), ((), ()))
NT = (((1,), (1,)), ((), ()))
VMEM_LIMIT = 48 * 2**20


class Layout:
    def __init__(self, size):
        bits = size.bit_length() - 1
        self.size = size
        self.partner_bits = [bits - 1, bits // 2, 0, 1]
        self.gate_bits = sorted(set(self.partner_bits))
        self.other_bits = [b for b in range(bits) if b not in self.gate_bits]
        self.local_bits = [self.gate_bits.index(b) for b in self.partner_bits]
        self.chips = 2 ** (len(self.gate_bits) - 1)

    def chip(self, index):
        return sum((index >> b & 1) << j for j, b in enumerate(self.gate_bits[1:]))

    def ring_position(self, chip):
        line, turn = chip >> 1, chip & 1
        return self.chips - 1 - line if turn else line

    def chip_at(self, position):
        position %= self.chips
        if position < self.chips // 2:
            return position << 1
        return (self.chips - 1 - position) << 1 | 1

    def shifted(self, index, step):
        chip = self.chip_at(self.ring_position(self.chip(index)) + step)
        for j, b in enumerate(self.gate_bits[1:]):
            index = index & ~(1 << b) | (chip >> j & 1) << b
        return index

    def ring(self, step):
        return [(i, self.shifted(i, step)) for i in range(self.size)]

    def flip(self, bit):
        return [(i, i ^ 1 << bit) for i in range(self.size)]

    def table(self):
        half = self.chips // 2
        steps = [0] + [s for k in range(1, half) for s in (-k, k)] + [half]
        low = self.gate_bits[0]
        return np.array(
            [[i >> low & 1] + [self.chip(self.shifted(i, s)) for s in steps] for i in range(self.size)], np.int32
        )


def gather_ring(block, layout):
    up, down = layout.ring(1), layout.ring(-1)
    half = layout.chips // 2
    from_below = from_above = block
    blocks = [block]
    for _ in range(1, half):
        from_below = lax.ppermute(from_below, "long", up)
        from_above = lax.ppermute(from_above, "long", down)
        blocks += [from_below, from_above]
    blocks += [lax.ppermute(from_below[:1], "long", up), lax.ppermute(from_above[1:], "long", down)]
    return blocks


def split(x):
    high = x.astype(BF16)
    return high, (x - high.astype(F32)).astype(BF16)


def dot(a, b, dims):
    return lax.dot_general(a, b, dims, preferred_element_type=F32)


def dot3(a, b, dims):
    return dot(a[0], b[0], dims) + (dot(a[0], b[1], dims) + dot(a[1], b[0], dims))


def turned(a):
    n = a.shape[1] // 2
    return jnp.concatenate([-a[:, n:], a[:, :n]], 1)


def as_matrix(a):
    n = a.shape[1] // 2
    return jnp.concatenate([jnp.concatenate([a[:, :n], -a[:, n:]], 1), jnp.concatenate([a[:, n:], a[:, :n]], 1)], 0)


def polar(e):
    x = e * lax.rsqrt(jnp.sum(e * e) + 1e-6)
    for _ in range(NS_ITERS):
        xs = split(x)
        rows = [jnp.concatenate([v, turned(v)], 0) for v in xs]
        h = dot3(xs, rows, NT)
        p = dot3(split(h), rows, NN)
        x = 1.5 * x - 0.5 * p
    return x


def pair_of(rest, bit):
    low = rest & ((1 << bit) - 1)
    first = (rest - low) * 2 + low
    return first, first + (1 << bit)


def load_pair(ref, rest, bit):
    d0, d1 = pair_of(rest, bit)
    return [
        jnp.concatenate([ref[k, d0, 0], ref[k, d1, 0], ref[k, d0, 1], ref[k, d1, 1]], 0) for k in range(2)
    ]


def store_pair(ref, rest, bit, y):
    d0, d1 = pair_of(rest, bit)
    n = y.shape[0] // 4
    for k, v in enumerate(split(y)):
        ref[k, d0, 0], ref[k, d1, 0] = v[:n], v[n : 2 * n]
        ref[k, d0, 1], ref[k, d1, 1] = v[2 * n : 3 * n], v[3 * n :]


def apply_gate(gate, source, target, bit):
    def body(rest, _):
        store_pair(target, rest, bit, dot3(gate, load_pair(source, rest, bit), NN))
        return 0

    lax.fori_loop(0, source.shape[1] // 2, body, 0, unroll=2)


def environment(phi, psi, bit):
    total = None
    for rest in range(psi.shape[1] // 2):
        term = dot3(load_pair(phi, rest, bit), load_pair(psi, rest, bit), NT)
        total = term if total is None else total + term
    n = total.shape[0] // 2
    return jnp.concatenate([total[:n, :n] + total[n:, n:], total[n:, :n] - total[:n, n:]], 1)


def place(table, blocks, target):
    core = table[0]
    for k in range(len(blocks) - 1):
        chip = table[1 + k]
        for slot in range(2):
            block = blocks[k + slot][0] if k == len(blocks) - 2 else blocks[k][slot]
            d = chip * 2 + (slot ^ core)
            target[0, d], target[1, d] = split(block)


def pack_kernel(table, x_ref, own_ref, sent_ref):
    core = table[0]
    n = x_ref.shape[2] // 2
    for plane in range(2):
        t = x_ref[plane].T
        low, high = t[:n], t[n:]
        own_ref[plane] = jnp.where(core == 0, low, high)
        sent_ref[plane] = jnp.where(core == 0, high, low)


def unpack_kernel(table, own_ref, got_ref, out_ref):
    core = table[0]
    for plane in range(2):
        own, got = own_ref[plane], got_ref[plane]
        low, high = jnp.where(core == 0, own, got), jnp.where(core == 0, got, own)
        out_ref[plane] = jnp.concatenate([low, high], 0).T


def adjoint_kernel(layout, table, gates_ref, *refs):
    *blocks, phis_ref, own_ref, sent_ref, first = refs
    place(table, blocks, first)
    source = first
    for s in range(SECTIONS):
        gate = as_matrix(jnp.concatenate([gates_ref[s, 0], gates_ref[s, 1]], 1))
        apply_gate(split(gate), source, phis_ref.at[s], layout.local_bits[s])
        source = phis_ref.at[s]
    core, chip = table[0], table[1]
    last = phis_ref.at[SECTIONS - 1]
    for slot, out in enumerate((own_ref, sent_ref)):
        d = chip * 2 + (slot ^ core)
        out[...] = last[0, d].astype(F32) + last[1, d].astype(F32)


def first_kernel(layout, table, phis_ref, *refs):
    *blocks, psi_ref, e_ref = refs
    place(table, blocks, psi_ref)
    e_ref[...] = environment(phis_ref.at[0], psi_ref, layout.local_bits[0])


def section_kernel(layout, section, e0_ref, e1_ref, phis_ref, psi_ref, next_ref, e_ref, phi, sem):
    copy = pltpu.make_async_copy(phis_ref.at[section + 1], phi, sem)
    copy.start()
    gate = split(as_matrix(polar(e0_ref[...] + e1_ref[...])))
    apply_gate(gate, psi_ref, next_ref, layout.local_bits[section])
    copy.wait()
    e_ref[...] = environment(phi, next_ref, layout.local_bits[section + 1])


def last_kernel(layout, table, e0_ref, e1_ref, psi_ref, own_ref, sent_ref, scratch):
    bit = layout.local_bits[SECTIONS - 1]
    scratch[...] = as_matrix(polar(e0_ref[...] + e1_ref[...]))
    core, chip = table[0], table[1]
    n = own_ref.shape[1]
    for slot, out in enumerate((own_ref, sent_ref)):
        d = chip * 2 + (slot ^ core)
        t = d >> bit & 1
        rest = (d >> bit + 1 << bit) + (d & (1 << bit) - 1)
        x = load_pair(psi_ref, rest, bit)
        for plane in range(2):
            start = pl.multiple_of(plane * 2 * n + t * n, n)
            out[plane] = dot3(split(scratch[pl.ds(start, n)]), x, NN)


SMEM = pl.BlockSpec(memory_space=pltpu.SMEM)
VMEM = pl.BlockSpec(memory_space=pltpu.VMEM)
ANY = pl.BlockSpec(memory_space=pl.ANY)


def call(kernel, name, outs, ins, specs, flops, scratch=()):
    sizes = [int(np.prod(a.shape)) * a.dtype.itemsize for a in list(ins) + list(outs)]
    return pl.pallas_call(
        kernel,
        out_shape=outs,
        in_specs=specs,
        out_specs=[VMEM] * len(outs),
        scratch_shapes=list(scratch),
        compiler_params=pltpu.CompilerParams(vmem_limit_bytes=VMEM_LIMIT),
        cost_estimate=pl.CostEstimate(flops=flops, bytes_accessed=sum(sizes), transcendentals=0),
        name=name,
    )(*ins)


def shards(initial_state, adjoint_state, current_gates):
    layout = Layout(lax.axis_size("long"))
    core_flip = layout.flip(layout.gate_bits[0])
    table = jnp.asarray(layout.table())[lax.axis_index("long")]
    rows, lanes = initial_state.shape[1:]
    c = lanes // 2
    devices = layout.chips * 2
    slab = jax.ShapeDtypeStruct((2, c, rows), F32)
    pieces = jax.ShapeDtypeStruct((2, devices, 2, c, rows), BF16)
    all_pieces = jax.ShapeDtypeStruct((SECTIONS,) + pieces.shape, BF16)
    env = jax.ShapeDtypeStruct((lanes, 2 * lanes), F32)
    apply_flops = 3 * 2 * (2 * lanes) ** 2 * (devices // 2) * rows

    def pack(x):
        own, sent = call(pack_kernel, "pack", [slab, slab], [table, x], [SMEM, VMEM], 0)
        return jnp.stack([own, lax.ppermute(sent, "long", core_flip)])

    def unpack(own, sent):
        got = lax.ppermute(sent, "long", core_flip)
        full = jax.ShapeDtypeStruct((2, rows, lanes), F32)
        return call(unpack_kernel, "unpack", [full], [table, own, got], [SMEM, VMEM, VMEM], 0)[0]

    def both(e):
        for bit in layout.other_bits:
            e = e + lax.ppermute(e, "long", layout.flip(bit))
        return e, lax.ppermute(e, "long", core_flip)

    phi_blocks = gather_ring(pack(adjoint_state), layout)
    psi_blocks = gather_ring(pack(initial_state), layout)
    phis, phi_own, phi_sent = call(
        functools.partial(adjoint_kernel, layout),
        "adjoint",
        [all_pieces, slab, slab],
        [table, current_gates] + phi_blocks,
        [SMEM] + [VMEM] * (1 + len(phi_blocks)),
        SECTIONS * apply_flops,
        [pltpu.VMEM(pieces.shape, BF16)],
    )
    final_adjoint = unpack(phi_own, phi_sent)
    psi, e = call(
        functools.partial(first_kernel, layout),
        "first",
        [pieces, env],
        [table, phis] + psi_blocks,
        [SMEM] + [VMEM] * (1 + len(psi_blocks)),
        apply_flops,
    )
    for section in range(SECTIONS - 1):
        e0, e1 = both(e)
        psi, e = call(
            functools.partial(section_kernel, layout, section),
            "section",
            [pieces, env],
            [e0, e1, phis, psi],
            [VMEM, VMEM, ANY, VMEM],
            3 * apply_flops,
            [pltpu.VMEM(pieces.shape, BF16), pltpu.SemaphoreType.DMA],
        )
    e0, e1 = both(e)
    own, sent = call(
        functools.partial(last_kernel, layout),
        "last",
        [slab, slab],
        [table, e0, e1, psi],
        [SMEM, VMEM, VMEM, VMEM],
        2 * apply_flops,
        [pltpu.VMEM((2 * lanes, 2 * lanes), F32)],
    )
    return unpack(own, sent), final_adjoint


def solution(mesh):
    return jax.shard_map(
        shards,
        mesh=mesh,
        in_specs=(
            P(None, ("groups", "long"), None),
            P(None, ("groups", "long"), None),
            P("groups", None, None, None),
        ),
        out_specs=(P(None, ("groups", "long"), None), P(None, ("groups", "long"), None)),
        check_vma=False,
    )
```

```python
import functools

import jax
import jax.numpy as jnp
import numpy as np
from jax import lax
from jax.experimental import pallas as pl
from jax.experimental.pallas import tpu as pltpu
from jax.sharding import PartitionSpec as P

SECTIONS = 4
NS_ITERS = 8

F32, BF16 = jnp.float32, jnp.bfloat16
NN = (((1,), (0,)), ((), ()))
NT = (((1,), (1,)), ((), ()))
VMEM_LIMIT = 24 * 2**20


class Layout:
    def __init__(self, size):
        bits = size.bit_length() - 1
        self.size = size
        self.partner_bits = [bits - 1, bits // 2, 0, 1]
        self.gate_bits = sorted(set(self.partner_bits))
        self.other_bits = [b for b in range(bits) if b not in self.gate_bits]
        self.local_bits = [self.gate_bits.index(b) for b in self.partner_bits]
        self.chips = 2 ** (len(self.gate_bits) - 1)

    def chip(self, index):
        return sum((index >> b & 1) << j for j, b in enumerate(self.gate_bits[1:]))

    def ring_position(self, chip):
        line, turn = chip >> 1, chip & 1
        return self.chips - 1 - line if turn else line

    def chip_at(self, position):
        position %= self.chips
        if position < self.chips // 2:
            return position << 1
        return (self.chips - 1 - position) << 1 | 1

    def shifted(self, index, step):
        chip = self.chip_at(self.ring_position(self.chip(index)) + step)
        for j, b in enumerate(self.gate_bits[1:]):
            index = index & ~(1 << b) | (chip >> j & 1) << b
        return index

    def ring(self, step):
        return [(i, self.shifted(i, step)) for i in range(self.size)]

    def flip(self, bit):
        return [(i, i ^ 1 << bit) for i in range(self.size)]

    def place_of(self, index):
        position = self.ring_position_traced(self.chip(index))
        half = self.chips // 2
        steps = [0] + [s for k in range(1, half) for s in (-k, k)] + [half]
        return index >> self.gate_bits[0] & 1, [self.chip_at_traced(position + s) for s in steps]

    def ring_position_traced(self, chip):
        line, turn = chip >> 1, chip & 1
        return jnp.where(turn == 1, self.chips - 1 - line, line)

    def chip_at_traced(self, position):
        position = position & self.chips - 1
        return jnp.where(position < self.chips // 2, position << 1, (self.chips - 1 - position) << 1 | 1)


def gather_ring(block, layout):
    up, down = layout.ring(1), layout.ring(-1)
    half = layout.chips // 2
    from_below = from_above = block
    blocks = [block]
    for _ in range(1, half):
        from_below = lax.ppermute(from_below, "long", up)
        from_above = lax.ppermute(from_above, "long", down)
        blocks += [from_below, from_above]
    blocks += [lax.ppermute(from_below[:1], "long", up), lax.ppermute(from_above[1:], "long", down)]
    return blocks


def split(x):
    high = x.astype(BF16)
    return high, (x - high.astype(F32)).astype(BF16)


def dot(a, b, dims):
    return lax.dot_general(a, b, dims, preferred_element_type=F32)


def dot3(a, b, dims):
    return dot(a[0], b[0], dims) + (dot(a[0], b[1], dims) + dot(a[1], b[0], dims))


def turned(a):
    n = a.shape[1] // 2
    return jnp.concatenate([-a[:, n:], a[:, :n]], 1)


def as_matrix(a):
    n = a.shape[1] // 2
    return jnp.concatenate([jnp.concatenate([a[:, :n], -a[:, n:]], 1), jnp.concatenate([a[:, n:], a[:, :n]], 1)], 0)


def polar(e, beside=lambda k: None):
    x = e * lax.rsqrt(jnp.sum(e * e) + 1e-6)
    for k in range(NS_ITERS):
        xs = split(x)
        rows = [jnp.concatenate([v, turned(v)], 0) for v in xs]
        h = dot3(xs, rows, NT)
        beside(k)
        p = dot3(split(h), rows, NN)
        x = 1.5 * x - 0.5 * p
    return x


def pair_of(rest, bit):
    low = rest & ((1 << bit) - 1)
    first = (rest - low) * 2 + low
    return first, first + (1 << bit)


def load_pair(ref, rest, bit):
    d0, d1 = pair_of(rest, bit)
    return [
        jnp.concatenate([ref[k, d0, 0], ref[k, d1, 0], ref[k, d0, 1], ref[k, d1, 1]], 0) for k in range(2)
    ]


def store_pair(ref, rest, bit, y):
    d0, d1 = pair_of(rest, bit)
    n = y.shape[0] // 4
    for k, v in enumerate(split(y)):
        ref[k, d0, 0], ref[k, d1, 0] = v[:n], v[n : 2 * n]
        ref[k, d0, 1], ref[k, d1, 1] = v[2 * n : 3 * n], v[3 * n :]


def apply_at(gate, source, target, bit, rest):
    store_pair(target, rest, bit, dot3(gate, load_pair(source, rest, bit), NN))


def folded(total):
    n = total.shape[0] // 2
    return jnp.concatenate([total[:n, :n] + total[n:, n:], total[n:, :n] - total[:n, n:]], 1)


def environment(phi, psi, bit, rests):
    terms = [dot3(load_pair(phi, rest, bit), load_pair(psi, rest, bit), NT) for rest in rests]
    return sum(terms[1:], terms[0])


def gate_matrix(gates_ref, section):
    return split(as_matrix(jnp.concatenate([gates_ref[section, 0], gates_ref[section, 1]], 1)))


def place(block, target, d):
    target[0, d], target[1, d] = split(block)


def joined(ref, d):
    return ref[0, d].astype(F32) + ref[1, d].astype(F32)


def unpacked(core, own, other, out_ref):
    for plane in range(2):
        low = jnp.where(core == 0, own[plane], other[plane])
        high = jnp.where(core == 0, other[plane], own[plane])
        out_ref[plane] = jnp.concatenate([low, high], 0).T


def pack_kernel(layout, x_ref, y_ref, x_own_ref, x_sent_ref, y_own_ref, y_sent_ref):
    core, _ = layout.place_of(lax.axis_index("long"))
    n = x_ref.shape[2] // 2
    for ref, own_ref, sent_ref in ((x_ref, x_own_ref, x_sent_ref), (y_ref, y_own_ref, y_sent_ref)):
        for plane in range(2):
            t = ref[plane].T
            low, high = t[:n], t[n:]
            own_ref[plane] = jnp.where(core == 0, low, high)
            sent_ref[plane] = jnp.where(core == 0, high, low)


def rests_of(layout, chip, bit):
    low = chip & (1 << bit - 1) - 1
    base = (chip >> bit << bit - 1) + low
    return [base * 2 + slot for slot in range(2)]


def near_kernel(layout, gates_ref, *refs):
    *blocks, phi_ref, psi_ref, total_ref, raw = refs
    core, chips = layout.place_of(lax.axis_index("long"))
    bit = layout.local_bits[0]
    half = len(blocks) // 2
    for source, target in ((blocks[:half], raw), (blocks[half:], psi_ref)):
        for block, chip in zip(source, chips):
            for slot in range(2):
                place(block[slot], target, chip * 2 + (slot ^ core))
    gate = gate_matrix(gates_ref, 0)
    far = chips[-1]
    others = [far ^ k for k in range(1, layout.chips) if not k >> bit - 1 & 1]
    rests = [r for chip in others for r in rests_of(layout, chip, bit)]
    for rest in rests:
        apply_at(gate, raw, phi_ref, bit, rest)
    total_ref[...] = environment(phi_ref, psi_ref, bit, rests)
    mate = (far ^ 1 << bit - 1) * 2
    for slot in range(2):
        for k in range(2):
            phi_ref[k, mate + slot] = raw[k, mate + slot]


def far_kernel(layout, gates_ref, *refs):
    *blocks, total_ref, phi_in, psi_in, phi_ref, psi_ref, e_ref = refs
    core, chips = layout.place_of(lax.axis_index("long"))
    bit = layout.local_bits[0]
    far = chips[-1]
    for source, target in ((blocks[:2], phi_ref), (blocks[2:], psi_ref)):
        for slot in range(2):
            place(source[slot][0], target, far * 2 + (slot ^ core))
    gate = gate_matrix(gates_ref, 0)
    rests = rests_of(layout, far, bit)
    for rest in rests:
        apply_at(gate, phi_ref, phi_ref, bit, rest)
    e_ref[...] = folded(total_ref[...] + environment(phi_ref, psi_ref, bit, rests))


def section_kernel(layout, section, gates_ref, e0_ref, e1_ref, phi_ref, psi_ref, phi_next, psi_next, e_ref, *ends):
    adjoint_gate = gate_matrix(gates_ref, section + 1)
    bit, next_bit = layout.local_bits[section], layout.local_bits[section + 1]
    rests = range(psi_ref.shape[1] // 2)

    def beside(k):
        for rest in rests[k * len(rests) // NS_ITERS : (k + 1) * len(rests) // NS_ITERS]:
            apply_at(adjoint_gate, phi_ref, phi_next, next_bit, rest)

    gate = split(as_matrix(polar(e0_ref[...] + e1_ref[...], beside)))
    for rest in rests:
        apply_at(gate, psi_ref, psi_next, bit, rest)
    e_ref[...] = folded(environment(phi_next, psi_next, next_bit, rests))
    if ends:
        core, chips = layout.place_of(lax.axis_index("long"))
        phi_own, phi_sent, psi_own, psi_sent = ends
        for slot, phi_out, psi_out in ((0, phi_own, psi_own), (1, phi_sent, psi_sent)):
            d = chips[0] * 2 + (slot ^ core)
            phi_out[...] = joined(phi_next, d)
            for t, d_t in enumerate(last_pair(layout, d)):
                psi_out[t] = joined(psi_next, d_t)


def last_pair(layout, d):
    bit = layout.local_bits[SECTIONS - 1]
    first = d & ~(1 << bit)
    return first, first + (1 << bit)


def last_polar_kernel(layout, e0_ref, e1_ref, phi_own, phi_got, gate_ref, adjoint_ref):
    core, _ = layout.place_of(lax.axis_index("long"))
    gate_ref[...] = as_matrix(polar(e0_ref[...] + e1_ref[...]))
    unpacked(core, phi_own, phi_got, adjoint_ref)


def last_apply_kernel(layout, gate_ref, psi_own, psi_got, state_ref):
    core, chips = layout.place_of(lax.axis_index("long"))
    t = chips[0] * 2 + core >> layout.local_bits[SECTIONS - 1] & 1
    n = psi_own.shape[2]
    rows = [gate_ref[pl.ds(pl.multiple_of((plane * 2 + t) * n, n), n)] for plane in range(2)]
    gate = split(jnp.concatenate(rows, 0))
    halves = []
    for psi in (psi_own, psi_got):
        x = jnp.concatenate([psi[0, 0], psi[1, 0], psi[0, 1], psi[1, 1]], 0)
        y = dot3(gate, split(x), NN)
        halves.append([y[:n], y[n:]])
    unpacked(core, halves[0], halves[1], state_ref)


def call(kernel, name, outs, ins, flops, scratch=(), aliases=None):
    sizes = [int(np.prod(a.shape)) * a.dtype.itemsize for a in list(ins) + list(outs)]
    spec = pl.BlockSpec(memory_space=pltpu.VMEM)
    return pl.pallas_call(
        kernel,
        out_shape=outs,
        in_specs=[spec] * len(ins),
        out_specs=[spec] * len(outs),
        scratch_shapes=list(scratch),
        input_output_aliases=aliases or {},
        compiler_params=pltpu.CompilerParams(vmem_limit_bytes=VMEM_LIMIT),
        cost_estimate=pl.CostEstimate(flops=flops, bytes_accessed=sum(sizes), transcendentals=0),
        name=name,
    )(*ins)


def shards(initial_state, adjoint_state, current_gates):
    layout = Layout(lax.axis_size("long"))
    core_flip = layout.flip(layout.gate_bits[0])
    rows, lanes = initial_state.shape[1:]
    c = lanes // 2
    devices = layout.chips * 2
    whole = jax.ShapeDtypeStruct(initial_state.shape, F32)
    slab = jax.ShapeDtypeStruct((2, c, rows), F32)
    two_slabs = jax.ShapeDtypeStruct((2, 2, c, rows), F32)
    pieces = jax.ShapeDtypeStruct((2, devices, 2, c, rows), BF16)
    env = jax.ShapeDtypeStruct((lanes, 2 * lanes), F32)
    square = jax.ShapeDtypeStruct((2 * lanes, 2 * lanes), F32)
    apply_flops = 3 * 2 * (2 * lanes) ** 2 * (devices // 2) * rows

    def kernel(body, *args):
        return functools.partial(body, layout, *args)

    def both(e):
        for bit in layout.other_bits:
            e = e + lax.ppermute(e, "long", layout.flip(bit))
        return e, lax.ppermute(e, "long", core_flip)

    phi_own, phi_sent, psi_own, psi_sent = call(
        kernel(pack_kernel), "pack", [slab] * 4, [adjoint_state, initial_state], 0
    )
    *phi_near, phi_a, phi_b = gather_ring(jnp.stack([phi_own, lax.ppermute(phi_sent, "long", core_flip)]), layout)
    *psi_near, psi_a, psi_b = gather_ring(jnp.stack([psi_own, lax.ppermute(psi_sent, "long", core_flip)]), layout)
    phi, psi, total = call(
        kernel(near_kernel),
        "near",
        [pieces, pieces, square],
        [current_gates] + phi_near + psi_near,
        2 * apply_flops,
        [pltpu.VMEM(pieces.shape, BF16)],
    )
    phi, psi, e = call(
        kernel(far_kernel),
        "far",
        [pieces, pieces, env],
        [current_gates, phi_a, phi_b, psi_a, psi_b, total, phi, psi],
        apply_flops // 2,
        aliases={6: 0, 7: 1},
    )
    for section in range(SECTIONS - 1):
        e0, e1 = both(e)
        ends = [slab, slab, two_slabs, two_slabs] if section == SECTIONS - 2 else []
        phi, psi, e, *ends = call(
            kernel(section_kernel, section),
            "section",
            [pieces, pieces, env] + ends,
            [current_gates, e0, e1, phi, psi],
            4 * apply_flops,
        )
    phi_own, phi_sent, psi_own, psi_sent = ends
    e0, e1 = both(e)
    phi_got = lax.ppermute(phi_sent, "long", core_flip)
    psi_got = lax.ppermute(psi_sent, "long", core_flip)
    gate, final_adjoint = call(
        kernel(last_polar_kernel), "last_polar", [square, whole], [e0, e1, phi_own, phi_got], 2 * apply_flops
    )
    (final_state,) = call(
        kernel(last_apply_kernel), "last_apply", [whole], [gate, psi_own, psi_got], apply_flops // 4
    )
    return final_state, final_adjoint


def solution(mesh):
    return jax.shard_map(
        shards,
        mesh=mesh,
        in_specs=(
            P(None, ("groups", "long"), None),
            P(None, ("groups", "long"), None),
            P("groups", None, None, None),
        ),
        out_specs=(P(None, ("groups", "long"), None), P(None, ("groups", "long"), None)),
        check_vma=False,
    )
```

```python
import functools

import jax
import jax.numpy as jnp
import numpy as np
from jax import lax
from jax.experimental import pallas as pl
from jax.experimental.pallas import tpu as pltpu
from jax.sharding import PartitionSpec as P

SECTIONS = 4
NS_ITERS = 8

F32, BF16 = jnp.float32, jnp.bfloat16
NN = (((1,), (0,)), ((), ()))
NT = (((1,), (1,)), ((), ()))
VMEM_LIMIT = 24 * 2**20


class Layout:
    def __init__(self, size):
        bits = size.bit_length() - 1
        self.size = size
        self.partner_bits = [bits - 1, bits // 2, 0, 1]
        self.gate_bits = sorted(set(self.partner_bits))
        self.other_bits = [b for b in range(bits) if b not in self.gate_bits]
        self.local_bits = [self.gate_bits.index(b) for b in self.partner_bits]
        self.chips = 2 ** (len(self.gate_bits) - 1)

    def chip(self, index):
        return sum((index >> b & 1) << j for j, b in enumerate(self.gate_bits[1:]))

    def ring_position(self, chip):
        line, turn = chip >> 1, chip & 1
        return self.chips - 1 - line if turn else line

    def chip_at(self, position):
        position %= self.chips
        if position < self.chips // 2:
            return position << 1
        return (self.chips - 1 - position) << 1 | 1

    def shifted(self, index, step):
        chip = self.chip_at(self.ring_position(self.chip(index)) + step)
        for j, b in enumerate(self.gate_bits[1:]):
            index = index & ~(1 << b) | (chip >> j & 1) << b
        return index

    def ring(self, step, flipped=0):
        return [(i, self.shifted(i, step) ^ flipped << self.gate_bits[0]) for i in range(self.size)]

    def flip(self, bit):
        return [(i, i ^ 1 << bit) for i in range(self.size)]

    def place_of(self, index):
        position = self.ring_position_traced(self.chip(index))
        half = self.chips // 2
        steps = [0] + [s for k in range(1, half) for s in (-k, k)] + [half]
        return index >> self.gate_bits[0] & 1, [self.chip_at_traced(position + s) for s in steps]

    def ring_position_traced(self, chip):
        line, turn = chip >> 1, chip & 1
        return jnp.where(turn == 1, self.chips - 1 - line, line)

    def chip_at_traced(self, position):
        position = position & self.chips - 1
        return jnp.where(position < self.chips // 2, position << 1, (self.chips - 1 - position) << 1 | 1)


def gather_ring(home, layout, before_last=lambda ends: ends):
    half = layout.chips // 2
    blocks, ends = [home], [home, home]
    for _ in range(1, half):
        ends = [lax.ppermute(end, "long", layout.ring(step)) for end, step in zip(ends, (1, -1))]
        blocks += ends
    ends = before_last(ends)
    opposite = [lax.ppermute(ends[k][k : k + 1], "long", layout.ring(1 - 2 * k)) for k in range(2)]
    return blocks, opposite


def split(x):
    high = x.astype(BF16)
    return high, (x - high.astype(F32)).astype(BF16)


def dot(a, b, dims):
    return lax.dot_general(a, b, dims, preferred_element_type=F32)


def dot3(a, b, dims):
    return dot(a[0], b[0], dims) + (dot(a[0], b[1], dims) + dot(a[1], b[0], dims))


def turned(a):
    n = a.shape[1] // 2
    return jnp.concatenate([-a[:, n:], a[:, :n]], 1)


def as_matrix(a):
    n = a.shape[1] // 2
    return jnp.concatenate([jnp.concatenate([a[:, :n], -a[:, n:]], 1), jnp.concatenate([a[:, n:], a[:, :n]], 1)], 0)


def polar(e):
    x = e * lax.rsqrt(jnp.sum(e * e) + 1e-6)
    for _ in range(NS_ITERS):
        xs = split(x)
        rows = [jnp.concatenate([v, turned(v)], 0) for v in xs]
        turns = [v[v.shape[0] // 2 :] for v in rows]
        h = split(jnp.concatenate([dot3(xs, xs, NT), dot3(xs, turns, NT)], 1))
        both = dot(jnp.concatenate(h, 0), rows[0], NN)
        n = x.shape[0]
        x = 1.5 * x - 0.5 * (both[:n] + both[n:] + dot(h[0], rows[1], NN))
    return x


def load_pair(ref, pair):
    return [jnp.concatenate([ref[k, d, plane] for plane in range(2) for d in pair], 0) for k in range(2)]


def store_pair(ref, pair, y):
    n = y.shape[0] // 4
    for k, v in enumerate(split(y)):
        for plane in range(2):
            for t, d in enumerate(pair):
                ref[k, d, plane] = v[(2 * plane + t) * n : (2 * plane + t + 1) * n]


def apply_at(gate, source, target, pair):
    store_pair(target, pair, dot3(gate, load_pair(source, pair), NN))


def folded(total):
    n = total.shape[0] // 2
    return jnp.concatenate([total[:n, :n] + total[n:, n:], total[n:, :n] - total[:n, n:]], 1)


def environment(phi, psi, pairs):
    terms = [dot3(load_pair(phi, pair), load_pair(psi, pair), NT) for pair in pairs]
    return sum(terms[1:], terms[0])


def gate_matrix(gates_ref, section):
    return split(as_matrix(jnp.concatenate([gates_ref[section, 0], gates_ref[section, 1]], 1)))


def place(block, target, d):
    target[0, d], target[1, d] = split(block)


def joined(ref, d):
    return ref[0, d].astype(F32) + ref[1, d].astype(F32)


def unpacked(core, own, other, out_ref):
    for plane in range(2):
        low = jnp.where(core == 0, own[plane], other[plane])
        high = jnp.where(core == 0, other[plane], own[plane])
        out_ref[plane] = jnp.concatenate([low, high], 0).T


def pack_kernel(layout, *refs):
    core, _ = layout.place_of(lax.axis_index("long"))
    n = refs[0].shape[2] // 2
    for x_ref, own_ref, sent_ref in ((refs[0], *refs[2:4]), (refs[1], *refs[4:6])):
        for plane in range(2):
            t = x_ref[plane].T
            low, high = t[:n], t[n:]
            own_ref[plane] = jnp.where(core == 0, low, high)
            sent_ref[plane] = jnp.where(core == 0, high, low)


TURN = 1


def all_pairs(layout, bit):
    return [(d, d + (1 << bit)) for d in range(2 * layout.chips) if not d >> bit & 1]


def line_pairs(layout, bit, turn):
    return [tuple(d + (turn << TURN) for d in pair) for pair in all_pairs(layout, bit) if not pair[0] >> TURN & 1]


def chip_pairs(bit, chip):
    firsts = [(chip * 2 + slot) & ~(1 << bit) for slot in range(2)]
    return [(d, d + (1 << bit)) for d in firsts]


def near_pairs(layout, far):
    bit = layout.local_bits[0]
    others = [far ^ k for k in range(1, layout.chips) if not k >> bit - 1 & 1]
    return [pair for chip in others for pair in chip_pairs(bit, chip)]


def place_blocks(blocks, chips, core, target):
    for block, chip in zip(blocks, chips):
        for slot in range(2):
            place(block[slot], target, chip * 2 + (slot ^ core))


def place_far(halves, chip, core, target):
    for slot in range(2):
        place(halves[slot][0], target, chip * 2 + (slot ^ core))


def line_kernel(layout, gates_ref, *refs):
    *blocks, phi0_ref, phi1_ref, phi2_ref = refs
    core, chips = layout.place_of(lax.axis_index("long"))
    place_blocks(blocks, chips, core, phi0_ref)
    gate = gate_matrix(gates_ref, 0)
    for pair in near_pairs(layout, chips[-1]):
        apply_at(gate, phi0_ref, phi0_ref, pair)
    for s, source, target in ((1, phi0_ref, phi1_ref), (2, phi1_ref, phi2_ref)):
        gate = gate_matrix(gates_ref, s)
        for pair in line_pairs(layout, layout.local_bits[s], chips[0] & 1):
            apply_at(gate, source, target, pair)


def near_kernel(layout, gates_ref, *refs):
    *blocks, phi_a, phi_b, phi_in, phi_ref, psi_ref, total_ref = refs
    core, chips = layout.place_of(lax.axis_index("long"))
    far = chips[-1]
    place_blocks(blocks, chips, core, psi_ref)
    total_ref[...] = environment(phi_ref, psi_ref, near_pairs(layout, far))
    place_far((phi_a, phi_b), far, core, phi_ref)
    gate = gate_matrix(gates_ref, 0)
    for pair in chip_pairs(layout.local_bits[0], far):
        apply_at(gate, phi_ref, phi_ref, pair)


def far_kernel(layout, psi_a, psi_b, total_ref, phi_ref, psi_in, psi_ref, e_ref):
    core, chips = layout.place_of(lax.axis_index("long"))
    far = chips[-1]
    place_far((psi_a, psi_b), far, core, psi_ref)
    e_ref[...] = folded(total_ref[...] + environment(phi_ref, psi_ref, chip_pairs(layout.local_bits[0], far)))


def other_line_kernel(layout, section, gates_ref, phi_ref, next_in, next_ref):
    _, chips = layout.place_of(lax.axis_index("long"))
    gate = gate_matrix(gates_ref, section)
    for pair in line_pairs(layout, layout.local_bits[section], 1 - (chips[0] & 1)):
        apply_at(gate, phi_ref, next_ref, pair)


def last_adjoint_kernel(layout, gates_ref, phi_ref, next_ref, own_ref, sent_ref):
    core, chips = layout.place_of(lax.axis_index("long"))
    gate = gate_matrix(gates_ref, SECTIONS - 1)
    for pair in all_pairs(layout, layout.local_bits[SECTIONS - 1]):
        apply_at(gate, phi_ref, next_ref, pair)
    for slot, out in enumerate((own_ref, sent_ref)):
        out[...] = joined(next_ref, chips[0] * 2 + (slot ^ core))


def ends_kernel(layout, psi_ref, own_ref, sent_ref):
    core, chips = layout.place_of(lax.axis_index("long"))
    for slot, out in enumerate((own_ref, sent_ref)):
        for t, d in enumerate(last_pair(layout, chips[0] * 2 + (slot ^ core))):
            out[t] = joined(psi_ref, d)


def section_kernel(layout, section, e0_ref, e1_ref, phi_ref, psi_ref, psi_next, e_ref):
    gate = split(as_matrix(polar(e0_ref[...] + e1_ref[...])))
    for pair in all_pairs(layout, layout.local_bits[section]):
        apply_at(gate, psi_ref, psi_next, pair)
    e_ref[...] = folded(environment(phi_ref, psi_next, all_pairs(layout, layout.local_bits[section + 1])))


def last_pair(layout, d):
    bit = layout.local_bits[SECTIONS - 1]
    first = d & ~(1 << bit)
    return first, first + (1 << bit)


def last_polar_kernel(layout, e0_ref, e1_ref, phi_own, phi_got, gate_ref, adjoint_ref):
    core, _ = layout.place_of(lax.axis_index("long"))
    gate_ref[...] = as_matrix(polar(e0_ref[...] + e1_ref[...]))
    unpacked(core, phi_own, phi_got, adjoint_ref)


def last_apply_kernel(layout, gate_ref, psi_own, psi_got, state_ref):
    core, chips = layout.place_of(lax.axis_index("long"))
    t = chips[0] * 2 + core >> layout.local_bits[SECTIONS - 1] & 1
    n = psi_own.shape[2]
    rows = [gate_ref[pl.ds(pl.multiple_of((plane * 2 + t) * n, n), n)] for plane in range(2)]
    gate = split(jnp.concatenate(rows, 0))
    halves = []
    for psi in (psi_own, psi_got):
        x = jnp.concatenate([psi[0, 0], psi[1, 0], psi[0, 1], psi[1, 1]], 0)
        y = dot3(gate, split(x), NN)
        halves.append([y[:n], y[n:]])
    unpacked(core, halves[0], halves[1], state_ref)


def call(kernel, name, outs, ins, flops, scratch=(), aliases=None):
    sizes = [int(np.prod(a.shape)) * a.dtype.itemsize for a in list(ins) + list(outs)]
    spec = pl.BlockSpec(memory_space=pltpu.VMEM)
    return pl.pallas_call(
        kernel,
        out_shape=outs,
        in_specs=[spec] * len(ins),
        out_specs=[spec] * len(outs),
        scratch_shapes=list(scratch),
        input_output_aliases=aliases or {},
        compiler_params=pltpu.CompilerParams(vmem_limit_bytes=VMEM_LIMIT),
        cost_estimate=pl.CostEstimate(flops=flops, bytes_accessed=sum(sizes), transcendentals=0),
        name=name,
    )(*ins)


def shards(initial_state, adjoint_state, current_gates):
    layout = Layout(lax.axis_size("long"))
    core_flip = layout.flip(layout.gate_bits[0])
    rows, lanes = initial_state.shape[1:]
    c = lanes // 2
    devices = layout.chips * 2
    whole = jax.ShapeDtypeStruct(initial_state.shape, F32)
    slab = jax.ShapeDtypeStruct((2, c, rows), F32)
    two_slabs = jax.ShapeDtypeStruct((2, 2, c, rows), F32)
    pieces = jax.ShapeDtypeStruct((2, devices, 2, c, rows), BF16)
    env = jax.ShapeDtypeStruct((lanes, 2 * lanes), F32)
    square = jax.ShapeDtypeStruct((2 * lanes, 2 * lanes), F32)
    apply_flops = 3 * 2 * (2 * lanes) ** 2 * (devices // 2) * rows

    def kernel(body, *args):
        return functools.partial(body, layout, *args)

    def both(e):
        for bit in layout.other_bits:
            e = e + lax.ppermute(e, "long", layout.flip(bit))
        return e, lax.ppermute(e, "long", core_flip)

    def home(own, sent):
        return jnp.stack([own, lax.ppermute(sent, "long", core_flip)])

    phi_own, phi_sent, psi_own, psi_sent = call(
        kernel(pack_kernel),
        "pack",
        [slab] * 4,
        [adjoint_state, initial_state],
        0,
    )
    phi_home = home(phi_own, phi_sent)
    phi_home, psi_own, psi_sent = lax.optimization_barrier((phi_home, psi_own, psi_sent))
    phi_near, phi_far = gather_ring(phi_home, layout)
    phis = list(
        call(kernel(line_kernel), "line", [pieces] * 3, [current_gates] + phi_near, 7 * apply_flops // 4)
    )

    def after_line(ends):
        return [ends[0], lax.optimization_barrier((ends[1], phis[0]))[0]]

    psi_near, psi_far = gather_ring(home(psi_own, psi_sent), layout, after_line)
    ins = [current_gates] + psi_near + phi_far + [phis[0]]
    phis[0], psi, total = call(
        kernel(near_kernel), "near", [pieces, pieces, square], ins, apply_flops, aliases={len(ins) - 1: 0}
    )
    psi, e = call(
        kernel(far_kernel), "far", [pieces, env], psi_far + [total, phis[0], psi], apply_flops // 4, aliases={4: 0}
    )
    for section in range(SECTIONS - 1):
        e0, e1 = both(e)
        if section < SECTIONS - 2:
            (phi,) = call(
                kernel(other_line_kernel, section + 1),
                "other_line",
                [pieces],
                [current_gates, phis[section], phis[section + 1]],
                apply_flops // 2,
                aliases={2: 0},
            )
            phis[section + 1] = phi
        else:
            phi, phi_own, phi_sent = call(
                kernel(last_adjoint_kernel),
                "last_adjoint",
                [pieces, slab, slab],
                [current_gates, phis[section]],
                apply_flops,
            )
        psi, e = call(kernel(section_kernel, section), "section", [pieces, env], [e0, e1, phi, psi], 3 * apply_flops)
    e0, e1 = both(e)
    psi_own, psi_sent = call(kernel(ends_kernel), "ends", [two_slabs, two_slabs], [psi], 0)
    phi_got = lax.ppermute(phi_sent, "long", core_flip)
    psi_got = lax.ppermute(psi_sent, "long", core_flip)
    gate, final_adjoint = call(
        kernel(last_polar_kernel), "last_polar", [square, whole], [e0, e1, phi_own, phi_got], 2 * apply_flops
    )
    (final_state,) = call(
        kernel(last_apply_kernel), "last_apply", [whole], [gate, psi_own, psi_got], apply_flops // 4
    )
    return final_state, final_adjoint


def solution(mesh):
    return jax.shard_map(
        shards,
        mesh=mesh,
        in_specs=(
            P(None, ("groups", "long"), None),
            P(None, ("groups", "long"), None),
            P("groups", None, None, None),
        ),
        out_specs=(P(None, ("groups", "long"), None), P(None, ("groups", "long"), None)),
        check_vma=False,
    )
```

```python
import functools

import jax
import jax.numpy as jnp
import numpy as np
from jax import lax
from jax.experimental import pallas as pl
from jax.experimental.pallas import tpu as pltpu
from jax.sharding import PartitionSpec as P

SECTIONS = 4
NS_ITERS = 8

F32, BF16 = jnp.float32, jnp.bfloat16
NN = (((1,), (0,)), ((), ()))
NT = (((1,), (1,)), ((), ()))
VMEM_LIMIT = 24 * 2**20


class Layout:
    def __init__(self, size):
        bits = size.bit_length() - 1
        self.size = size
        self.partner_bits = [bits - 1, bits // 2, 0, 1]
        self.gate_bits = sorted(set(self.partner_bits))
        self.other_bits = [b for b in range(bits) if b not in self.gate_bits]
        self.local_bits = [self.gate_bits.index(b) for b in self.partner_bits]
        self.chips = 2 ** (len(self.gate_bits) - 1)

    def chip(self, index):
        return sum((index >> b & 1) << j for j, b in enumerate(self.gate_bits[1:]))

    def ring_position(self, chip):
        line, turn = chip >> 1, chip & 1
        return self.chips - 1 - line if turn else line

    def chip_at(self, position):
        position %= self.chips
        if position < self.chips // 2:
            return position << 1
        return (self.chips - 1 - position) << 1 | 1

    def shifted(self, index, step):
        chip = self.chip_at(self.ring_position(self.chip(index)) + step)
        for j, b in enumerate(self.gate_bits[1:]):
            index = index & ~(1 << b) | (chip >> j & 1) << b
        return index

    def ring(self, step):
        return [(i, self.shifted(i, step)) for i in range(self.size)]

    def flip(self, bit):
        return [(i, i ^ 1 << bit) for i in range(self.size)]

    def place_of(self, index):
        position = self.ring_position_traced(self.chip(index))
        half = self.chips // 2
        steps = [0] + [s for k in range(1, half) for s in (-k, k)] + [half]
        return index >> self.gate_bits[0] & 1, [self.chip_at_traced(position + s) for s in steps]

    def ring_position_traced(self, chip):
        line, turn = chip >> 1, chip & 1
        return jnp.where(turn == 1, self.chips - 1 - line, line)

    def chip_at_traced(self, position):
        position = position & self.chips - 1
        return jnp.where(position < self.chips // 2, position << 1, (self.chips - 1 - position) << 1 | 1)


STEPS = (1, -1)


def gather_ring(home, layout):
    blocks, ends = [home], [home, home]
    for _ in range(1, layout.chips // 2):
        ends = [lax.ppermute(end, "long", layout.ring(step)) for end, step in zip(ends, STEPS)]
        blocks += ends
    return blocks, [ends[0][:1], ends[1][1:]]


def last_step(tail, layout):
    return [lax.ppermute(end, "long", layout.ring(step)) for end, step in zip(tail, STEPS)]


def split(x):
    high = x.astype(BF16)
    return high, (x - high.astype(F32)).astype(BF16)


def dot(a, b, dims):
    return lax.dot_general(a, b, dims, preferred_element_type=F32)


def dot3(a, b, dims):
    return dot(a[0], b[0], dims) + (dot(a[0], b[1], dims) + dot(a[1], b[0], dims))


def turned(a):
    n = a.shape[1] // 2
    return jnp.concatenate([-a[:, n:], a[:, :n]], 1)


def as_matrix(a):
    n = a.shape[1] // 2
    return jnp.concatenate([jnp.concatenate([a[:, :n], -a[:, n:]], 1), jnp.concatenate([a[:, n:], a[:, :n]], 1)], 0)


def polar(e, beside=lambda gap: None):
    x = e * lax.rsqrt(jnp.sum(e * e) + 1e-6)
    n = x.shape[0]
    for k in range(NS_ITERS):
        xs = split(x)
        turns = [turned(v) for v in xs]
        beside(2 * k)
        h = split(jnp.concatenate([dot3(xs, xs, NT), dot3(xs, turns, NT)], 1))
        beside(2 * k + 1)
        rows = [jnp.concatenate(pair, 0) for pair in zip(xs, turns)]
        both = dot(jnp.concatenate(h, 0), rows[0], NN)
        x = 1.5 * x - 0.5 * (both[:n] + both[n:] + dot(h[0], rows[1], NN))
    return x


def load_pair(ref, pair):
    return [jnp.concatenate([ref[k, d, plane] for plane in range(2) for d in pair], 0) for k in range(2)]


def store_pair(ref, pair, y):
    n = y.shape[0] // 4
    for k, v in enumerate(split(y)):
        for plane in range(2):
            for t, d in enumerate(pair):
                ref[k, d, plane] = v[(2 * plane + t) * n : (2 * plane + t + 1) * n]


def apply_at(gate, source, target, pair):
    store_pair(target, pair, dot3(gate, load_pair(source, pair), NN))


def folded(total):
    n = total.shape[0] // 2
    return jnp.concatenate([total[:n, :n] + total[n:, n:], total[n:, :n] - total[:n, n:]], 1)


def environment(phi, psi, pairs):
    terms = [dot3(load_pair(phi, pair), load_pair(psi, pair), NT) for pair in pairs]
    return sum(terms[1:], terms[0])


def gate_matrix(gates_ref, section):
    return split(as_matrix(jnp.concatenate([gates_ref[section, 0], gates_ref[section, 1]], 1)))


def place(block, target, d):
    target[0, d], target[1, d] = split(block)


def joined(ref, d):
    return ref[0, d].astype(F32) + ref[1, d].astype(F32)


def unpacked(core, own, other, out_ref):
    for plane in range(2):
        low = jnp.where(core == 0, own[plane], other[plane])
        high = jnp.where(core == 0, other[plane], own[plane])
        out_ref[plane] = jnp.concatenate([low, high], 0).T


def pack_kernel(layout, x_ref, own_ref, sent_ref):
    core, _ = layout.place_of(lax.axis_index("long"))
    n = x_ref.shape[2] // 2
    for plane in range(2):
        t = x_ref[plane].T
        low, high = t[:n], t[n:]
        own_ref[plane] = jnp.where(core == 0, low, high)
        sent_ref[plane] = jnp.where(core == 0, high, low)


TURN = 1


def all_pairs(layout, bit):
    return [(d, d + (1 << bit)) for d in range(2 * layout.chips) if not d >> bit & 1]


def line_pairs(layout, bit, turn):
    return [tuple(d + (turn << TURN) for d in pair) for pair in all_pairs(layout, bit) if not pair[0] >> TURN & 1]


def chip_pairs(bit, chip):
    firsts = [(chip * 2 + slot) & ~(1 << bit) for slot in range(2)]
    return [(d, d + (1 << bit)) for d in firsts]


def near_pairs(layout, far):
    bit = layout.local_bits[0]
    others = [far ^ k for k in range(1, layout.chips) if not k >> bit - 1 & 1]
    return [pair for chip in others for pair in chip_pairs(bit, chip)]


def place_blocks(blocks, chips, core, target):
    for block, chip in zip(blocks, chips):
        for slot in range(2):
            place(block[slot], target, chip * 2 + (slot ^ core))


def place_far(halves, chip, core, target):
    for slot in range(2):
        place(halves[slot][0], target, chip * 2 + (slot ^ core))


def first_gate_kernel(layout, gates_ref, *refs):
    *blocks, phi_ref = refs
    core, chips = layout.place_of(lax.axis_index("long"))
    place_blocks(blocks, chips, core, phi_ref)
    gate = gate_matrix(gates_ref, 0)
    for pair in near_pairs(layout, chips[-1]):
        apply_at(gate, phi_ref, phi_ref, pair)


def line_kernel(layout, gates_ref, phi0_ref, phi1_ref, phi2_ref):
    _, chips = layout.place_of(lax.axis_index("long"))
    for s, source, target in ((1, phi0_ref, phi1_ref), (2, phi1_ref, phi2_ref)):
        gate = gate_matrix(gates_ref, s)
        for pair in line_pairs(layout, layout.local_bits[s], chips[0] & 1):
            apply_at(gate, source, target, pair)


def near_kernel(layout, gates_ref, *refs):
    *blocks, phi_a, phi_b, phi_in, phi_ref, psi_ref, total_ref = refs
    core, chips = layout.place_of(lax.axis_index("long"))
    far = chips[-1]
    place_blocks(blocks, chips, core, psi_ref)
    total_ref[...] = environment(phi_ref, psi_ref, near_pairs(layout, far))
    place_far((phi_a, phi_b), far, core, phi_ref)
    gate = gate_matrix(gates_ref, 0)
    for pair in chip_pairs(layout.local_bits[0], far):
        apply_at(gate, phi_ref, phi_ref, pair)


def far_kernel(layout, psi_a, psi_b, total_ref, phi_ref, psi_in, psi_ref, e_ref):
    core, chips = layout.place_of(lax.axis_index("long"))
    far = chips[-1]
    place_far((psi_a, psi_b), far, core, psi_ref)
    e_ref[...] = folded(total_ref[...] + environment(phi_ref, psi_ref, chip_pairs(layout.local_bits[0], far)))


def other_line_kernel(layout, section, gates_ref, phi_ref, next_in, next_ref):
    _, chips = layout.place_of(lax.axis_index("long"))
    gate = gate_matrix(gates_ref, section)
    for pair in line_pairs(layout, layout.local_bits[section], 1 - (chips[0] & 1)):
        apply_at(gate, phi_ref, next_ref, pair)


def last_adjoint_kernel(layout, gates_ref, phi_ref, next_ref, own_ref, sent_ref):
    core, chips = layout.place_of(lax.axis_index("long"))
    gate = gate_matrix(gates_ref, SECTIONS - 1)
    for pair in all_pairs(layout, layout.local_bits[SECTIONS - 1]):
        apply_at(gate, phi_ref, next_ref, pair)
    for slot, out in enumerate((own_ref, sent_ref)):
        out[...] = joined(next_ref, chips[0] * 2 + (slot ^ core))


def last_pair(layout, d):
    bit = layout.local_bits[SECTIONS - 1]
    first = d & ~(1 << bit)
    return first, first + (1 << bit)


def insert_bits(rest, bits):
    for bit in sorted(bits):
        rest = (rest >> bit << bit + 1) + (rest & (1 << bit) - 1)
    return rest


def load_quad(ref, rest, bits, plane):
    d = insert_bits(rest, bits)
    quad = [d + (t1 << bits[0]) + (t0 << bits[1]) for t1 in range(2) for t0 in range(2)]
    return [jnp.concatenate([ref[k, q, plane] for q in quad], 0) for k in range(2)]


def section_kernel(layout, section, e0_ref, e1_ref, phi_ref, psi_ref, gate_ref, e_ref, joint, left):
    bits = layout.local_bits[section + 1], layout.local_bits[section]
    rests = psi_ref.shape[1] // 4
    q = joint.shape[0] // 2
    c = q // 4
    units = [(rest, p, u) for rest in range(rests) for p in range(2) for u in range(2)]
    gaps = 2 * NS_ITERS - 2

    def add(rest, p, u):
        term = dot3(load_quad(phi_ref, rest, bits, p), load_quad(psi_ref, rest, bits, u), NT)
        at = (slice(p * q, p * q + q), slice(u * q, u * q + q))
        joint[at] = term if rest == 0 else joint[at] + term

    def arrange(p):
        real = joint[:q, :q] + joint[q:, q:] if p == 0 else joint[q:, :q] - joint[:q, q:]
        for k, v in enumerate(split(real)):
            for u1 in range(2):
                for t1 in range(2):
                    for t0 in range(2):
                        rows = slice((u1 * 2 + t1) * c, (u1 * 2 + t1 + 1) * c)
                        lanes = slice((p * 2 + t0) * 2 * c, (p * 2 + t0 + 1) * 2 * c)
                        left[k, rows, lanes] = v[(t1 * 2 + t0) * c : (t1 * 2 + t0 + 1) * c, u1 * 2 * c : (u1 + 1) * 2 * c]

    def beside(gap):
        for unit in units[gap * len(units) // gaps : (gap + 1) * len(units) // gaps] if gap < gaps else ():
            add(*unit)
        if gap >= gaps:
            arrange(gap - gaps)

    x = polar(e0_ref[...] + e1_ref[...], beside)
    right = []
    for v in split(x):
        r0, r1, i0, i1 = v[:c, : 2 * c], v[c:, : 2 * c], v[:c, 2 * c :], v[c:, 2 * c :]
        right.append(
            jnp.concatenate([jnp.concatenate([r0, r1, i0, i1], 1), jnp.concatenate([-i0, -i1, r0, r1], 1)], 0)
        )
    out = dot3((left[0], left[1]), right, NT)
    first, second = out[: 2 * c], out[2 * c :]
    e_ref[...] = jnp.concatenate([first[:, :c], second[:, :c], first[:, c:], second[:, c:]], 1)
    gate_ref[0], gate_ref[1] = split(as_matrix(x))


def apply_kernel(layout, section, gate_ref, psi_ref, next_ref):
    gate = gate_ref[0], gate_ref[1]
    for pair in all_pairs(layout, layout.local_bits[section]):
        apply_at(gate, psi_ref, next_ref, pair)


def ends_kernel(layout, gate_ref, psi_ref, own_ref, sent_ref):
    core, chips = layout.place_of(lax.axis_index("long"))
    gate = gate_ref[0], gate_ref[1]
    n = own_ref.shape[2]
    for t, first in enumerate(last_pair(layout, chips[0] * 2)):
        y = dot3(gate, load_pair(psi_ref, (first, first + 1)), NN)
        for plane in range(2):
            low, high = y[2 * plane * n : (2 * plane + 1) * n], y[(2 * plane + 1) * n : (2 * plane + 2) * n]
            own_ref[t, plane] = jnp.where(core == 0, low, high)
            sent_ref[t, plane] = jnp.where(core == 0, high, low)


def last_polar_kernel(e0_ref, e1_ref, gate_ref):
    gate_ref[...] = as_matrix(polar(e0_ref[...] + e1_ref[...]))


def unpack_kernel(layout, own_ref, got_ref, out_ref):
    core, _ = layout.place_of(lax.axis_index("long"))
    unpacked(core, own_ref, got_ref, out_ref)


def last_apply_kernel(layout, gate_ref, psi_own, psi_got, state_ref):
    core, chips = layout.place_of(lax.axis_index("long"))
    t = chips[0] * 2 + core >> layout.local_bits[SECTIONS - 1] & 1
    n = psi_own.shape[2]
    rows = [gate_ref[pl.ds(pl.multiple_of((plane * 2 + t) * n, n), n)] for plane in range(2)]
    gate = split(jnp.concatenate(rows, 0))
    halves = []
    for psi in (psi_own, psi_got):
        x = jnp.concatenate([psi[0, 0], psi[1, 0], psi[0, 1], psi[1, 1]], 0)
        y = dot3(gate, split(x), NN)
        halves.append([y[:n], y[n:]])
    unpacked(core, halves[0], halves[1], state_ref)


def call(kernel, name, outs, ins, flops, scratch=(), aliases=None):
    sizes = [int(np.prod(a.shape)) * a.dtype.itemsize for a in list(ins) + list(outs)]
    spec = pl.BlockSpec(memory_space=pltpu.VMEM)
    return pl.pallas_call(
        kernel,
        out_shape=outs,
        in_specs=[spec] * len(ins),
        out_specs=[spec] * len(outs),
        scratch_shapes=list(scratch),
        input_output_aliases=aliases or {},
        compiler_params=pltpu.CompilerParams(vmem_limit_bytes=VMEM_LIMIT),
        cost_estimate=pl.CostEstimate(flops=flops, bytes_accessed=sum(sizes), transcendentals=0),
        name=name,
    )(*ins)


def shards(initial_state, adjoint_state, current_gates):
    layout = Layout(lax.axis_size("long"))
    core_flip = layout.flip(layout.gate_bits[0])
    rows, lanes = initial_state.shape[1:]
    c = lanes // 2
    devices = layout.chips * 2
    whole = jax.ShapeDtypeStruct(initial_state.shape, F32)
    slab = jax.ShapeDtypeStruct((2, c, rows), F32)
    two_slabs = jax.ShapeDtypeStruct((2, 2, c, rows), F32)
    pieces = jax.ShapeDtypeStruct((2, devices, 2, c, rows), BF16)
    env = jax.ShapeDtypeStruct((lanes, 2 * lanes), F32)
    square = jax.ShapeDtypeStruct((2 * lanes, 2 * lanes), F32)
    apply_flops = 3 * 2 * (2 * lanes) ** 2 * (devices // 2) * rows

    def kernel(body, *args):
        return functools.partial(body, layout, *args)

    def both(e):
        for bit in layout.other_bits:
            e = e + lax.ppermute(e, "long", layout.flip(bit))
        return e, lax.ppermute(e, "long", core_flip)

    def home(own, sent):
        return jnp.stack([own, lax.ppermute(sent, "long", core_flip)])

    def pack(state):
        return call(kernel(pack_kernel), "pack", [slab] * 2, [state], 0)

    def after(x, *others):
        return lax.optimization_barrier((x, *others))[0]

    phi_home = home(*pack(adjoint_state))
    psi_own, psi_sent = pack(initial_state)
    phi_home, psi_own, psi_sent = lax.optimization_barrier((phi_home, psi_own, psi_sent))
    phi_near, phi_tail = gather_ring(phi_home, layout)
    phis = [call(kernel(first_gate_kernel), "first_gate", [pieces], [current_gates] + phi_near, apply_flops)[0]]
    phi_far = last_step(phi_tail, layout)
    phis += call(kernel(line_kernel), "line", [pieces] * 2, [current_gates, phis[0]], apply_flops)
    psi_near, psi_tail = gather_ring(home(psi_own, psi_sent), layout)
    psi_far = last_step([psi_tail[0], after(psi_tail[1], phis[1])], layout)
    ins = [current_gates] + psi_near + phi_far + [phis[0]]
    phis[0], psi, total = call(
        kernel(near_kernel), "near", [pieces, pieces, square], ins, apply_flops, aliases={len(ins) - 1: 0}
    )

    def other_line(section):
        ins = [current_gates, phis[section - 1], phis[section]]
        return call(
            kernel(other_line_kernel, section), "other_line", [pieces], ins, apply_flops // 2, aliases={2: 0}
        )[0]

    phis[1] = other_line(1)
    phis[2] = other_line(2)
    total = after(total, phis[2])
    psi, e = call(
        kernel(far_kernel), "far", [pieces, env], psi_far + [total, phis[0], psi], apply_flops // 4, aliases={4: 0}
    )
    gate_pair = jax.ShapeDtypeStruct((2,) + square.shape, BF16)
    for section in range(SECTIONS - 1):
        e0, e1 = both(e)
        if section == 0:
            phi, phi_own, phi_sent = call(
                kernel(last_adjoint_kernel),
                "last_adjoint",
                [pieces, slab, slab],
                [current_gates, phis[2]],
                apply_flops,
            )
            phis.append(phi)
            psi = after(psi, phi)
        else:
            (psi,) = call(kernel(apply_kernel, section - 1), "apply", [pieces], [gate, psi], apply_flops)
        if section == 1:
            phi_got = lax.ppermute(after(phi_sent, e), "long", core_flip)
        gate, e = call(
            kernel(section_kernel, section),
            "section",
            [gate_pair, env],
            [e0, e1, phis[section + 1], psi],
            4 * apply_flops,
            [pltpu.VMEM((4 * lanes, 4 * lanes), F32), pltpu.VMEM((2, 2 * lanes, 4 * lanes), BF16)],
        )
    e0, e1 = both(e)
    psi_own, psi_sent = call(kernel(ends_kernel), "ends", [two_slabs, two_slabs], [gate, psi], apply_flops // 4)
    psi_got = lax.ppermute(psi_sent, "long", core_flip)
    (final_adjoint,) = call(kernel(unpack_kernel), "unpack", [whole], [after(phi_own, e), phi_got], 0)
    (gate,) = call(last_polar_kernel, "last_polar", [square], [e0, e1], 2 * apply_flops)
    (final_state,) = call(
        kernel(last_apply_kernel), "last_apply", [whole], [gate, psi_own, psi_got], apply_flops // 4
    )
    return final_state, final_adjoint


def solution(mesh):
    return jax.shard_map(
        shards,
        mesh=mesh,
        in_specs=(
            P(None, ("groups", "long"), None),
            P(None, ("groups", "long"), None),
            P("groups", None, None, None),
        ),
        out_specs=(P(None, ("groups", "long"), None), P(None, ("groups", "long"), None)),
        check_vma=False,
    )
```

```python
import functools

import jax
import jax.numpy as jnp
import numpy as np
from jax import lax
from jax.experimental import pallas as pl
from jax.experimental.pallas import tpu as pltpu
from jax.sharding import PartitionSpec as P

SECTIONS = 4
NS_ITERS = 8

F32, BF16 = jnp.float32, jnp.bfloat16
NN = (((1,), (0,)), ((), ()))
NT = (((1,), (1,)), ((), ()))
VMEM_LIMIT = 24 * 2**20


class Layout:
    def __init__(self, size):
        bits = size.bit_length() - 1
        self.size = size
        self.partner_bits = [bits - 1, bits // 2, 0, 1]
        self.gate_bits = sorted(set(self.partner_bits))
        self.other_bits = [b for b in range(bits) if b not in self.gate_bits]
        self.local_bits = [self.gate_bits.index(b) for b in self.partner_bits]
        self.chips = 2 ** (len(self.gate_bits) - 1)

    def chip(self, index):
        return sum((index >> b & 1) << j for j, b in enumerate(self.gate_bits[1:]))

    def ring_position(self, chip):
        line, turn = chip >> 1, chip & 1
        return self.chips - 1 - line if turn else line

    def chip_at(self, position):
        position %= self.chips
        if position < self.chips // 2:
            return position << 1
        return (self.chips - 1 - position) << 1 | 1

    def shifted(self, index, step):
        chip = self.chip_at(self.ring_position(self.chip(index)) + step)
        for j, b in enumerate(self.gate_bits[1:]):
            index = index & ~(1 << b) | (chip >> j & 1) << b
        return index

    def ring(self, step):
        return [(i, self.shifted(i, step)) for i in range(self.size)]

    def flip(self, bit):
        return [(i, i ^ 1 << bit) for i in range(self.size)]

    def place_of(self, index):
        position = self.ring_position_traced(self.chip(index))
        half = self.chips // 2
        steps = [0] + [s for k in range(1, half) for s in (-k, k)] + [half]
        return index >> self.gate_bits[0] & 1, [self.chip_at_traced(position + s) for s in steps]

    def ring_position_traced(self, chip):
        line, turn = chip >> 1, chip & 1
        return jnp.where(turn == 1, self.chips - 1 - line, line)

    def chip_at_traced(self, position):
        position = position & self.chips - 1
        return jnp.where(position < self.chips // 2, position << 1, (self.chips - 1 - position) << 1 | 1)


STEPS = (1, -1)


def gather_ring(home, layout):
    blocks, ends = [home], [home, home]
    for _ in range(1, layout.chips // 2):
        ends = [lax.ppermute(end, "long", layout.ring(step)) for end, step in zip(ends, STEPS)]
        blocks += ends
    return blocks, [ends[0][:1], ends[1][1:]]


def last_step(tail, layout):
    return [lax.ppermute(end, "long", layout.ring(step)) for end, step in zip(tail, STEPS)]


def split(x):
    high = x.astype(BF16)
    return high, (x - high.astype(F32)).astype(BF16)


def dot(a, b, dims):
    return lax.dot_general(a, b, dims, preferred_element_type=F32)


def dot3(a, b, dims):
    return dot(a[0], b[0], dims) + (dot(a[0], b[1], dims) + dot(a[1], b[0], dims))


def turned(a):
    n = a.shape[1] // 2
    return jnp.concatenate([-a[:, n:], a[:, :n]], 1)


def as_matrix(a):
    n = a.shape[1] // 2
    return jnp.concatenate([jnp.concatenate([a[:, :n], -a[:, n:]], 1), jnp.concatenate([a[:, n:], a[:, :n]], 1)], 0)


def polar(e, beside=lambda gap: None):
    x = e * lax.rsqrt(jnp.sum(e * e) + 1e-6)
    n = x.shape[0]
    for k in range(NS_ITERS):
        xs = split(x)
        turns = [turned(v) for v in xs]
        beside(2 * k)
        h = split(jnp.concatenate([dot3(xs, xs, NT), dot3(xs, turns, NT)], 1))
        beside(2 * k + 1)
        rows = [jnp.concatenate(pair, 0) for pair in zip(xs, turns)]
        both = dot(jnp.concatenate(h, 0), rows[0], NN)
        x = 1.5 * x - 0.5 * (both[:n] + both[n:] + dot(h[0], rows[1], NN))
    return x


def load_pair(ref, pair):
    return [jnp.concatenate([ref[k, d, plane] for plane in range(2) for d in pair], 0) for k in range(2)]


def store_pair(ref, pair, y):
    n = y.shape[0] // 4
    for k, v in enumerate(split(y)):
        for plane in range(2):
            for t, d in enumerate(pair):
                ref[k, d, plane] = v[(2 * plane + t) * n : (2 * plane + t + 1) * n]


def apply_at(gate, source, target, pair):
    store_pair(target, pair, dot3(gate, load_pair(source, pair), NN))


def folded(total):
    n = total.shape[0] // 2
    return jnp.concatenate([total[:n, :n] + total[n:, n:], total[n:, :n] - total[:n, n:]], 1)


def environment(phi, psi, pairs):
    terms = [dot3(load_pair(phi, pair), load_pair(psi, pair), NT) for pair in pairs]
    return sum(terms[1:], terms[0])


def gate_matrix(gates_ref, section):
    return split(as_matrix(jnp.concatenate([gates_ref[section, 0], gates_ref[section, 1]], 1)))


def place(block, target, d):
    target[0, d], target[1, d] = split(block)


def joined(ref, d):
    return ref[0, d].astype(F32) + ref[1, d].astype(F32)


def unpacked(core, own, other):
    return jnp.concatenate([jnp.where(core == 0, own, other), jnp.where(core == 0, other, own)], 0).T


def pack_kernel(layout, x_ref, own_ref, sent_ref):
    core, _ = layout.place_of(lax.axis_index("long"))
    n = x_ref.shape[2] // 2
    for plane in range(2):
        t = x_ref[plane].T
        low, high = t[:n], t[n:]
        own_ref[plane] = jnp.where(core == 0, low, high)
        sent_ref[plane] = jnp.where(core == 0, high, low)


TURN = 1


def all_pairs(layout, bit):
    return [(d, d + (1 << bit)) for d in range(2 * layout.chips) if not d >> bit & 1]


def line_pairs(layout, bit, turn):
    return [tuple(d + (turn << TURN) for d in pair) for pair in all_pairs(layout, bit) if not pair[0] >> TURN & 1]


def chip_pairs(bit, chip):
    firsts = [(chip * 2 + slot) & ~(1 << bit) for slot in range(2)]
    return [(d, d + (1 << bit)) for d in firsts]


def near_pairs(layout, far):
    bit = layout.local_bits[0]
    others = [far ^ k for k in range(1, layout.chips) if not k >> bit - 1 & 1]
    return [pair for chip in others for pair in chip_pairs(bit, chip)]


def place_blocks(blocks, chips, core, target):
    for block, chip in zip(blocks, chips):
        for slot in range(2):
            place(block[slot], target, chip * 2 + (slot ^ core))


def place_far(halves, chip, core, target):
    for slot in range(2):
        place(halves[slot][0], target, chip * 2 + (slot ^ core))


def first_gate_kernel(layout, gates_ref, *refs):
    *blocks, phi_ref = refs
    core, chips = layout.place_of(lax.axis_index("long"))
    place_blocks(blocks, chips, core, phi_ref)
    gate = gate_matrix(gates_ref, 0)
    for pair in near_pairs(layout, chips[-1]):
        apply_at(gate, phi_ref, phi_ref, pair)


def line_kernel(layout, gates_ref, phi0_ref, phi1_ref, phi2_ref):
    _, chips = layout.place_of(lax.axis_index("long"))
    for s, source, target in ((1, phi0_ref, phi1_ref), (2, phi1_ref, phi2_ref)):
        gate = gate_matrix(gates_ref, s)
        for pair in line_pairs(layout, layout.local_bits[s], chips[0] & 1):
            apply_at(gate, source, target, pair)


def near_kernel(layout, gates_ref, *refs):
    *blocks, phi_a, phi_b, phi_in, phi_ref, psi_ref, total_ref = refs
    core, chips = layout.place_of(lax.axis_index("long"))
    far = chips[-1]
    place_blocks(blocks, chips, core, psi_ref)
    total_ref[...] = environment(phi_ref, psi_ref, near_pairs(layout, far))
    place_far((phi_a, phi_b), far, core, phi_ref)
    gate = gate_matrix(gates_ref, 0)
    for pair in chip_pairs(layout.local_bits[0], far):
        apply_at(gate, phi_ref, phi_ref, pair)


def far_kernel(layout, psi_a, psi_b, total_ref, phi_ref, psi_in, psi_ref, e_ref):
    core, chips = layout.place_of(lax.axis_index("long"))
    far = chips[-1]
    place_far((psi_a, psi_b), far, core, psi_ref)
    e_ref[...] = folded(total_ref[...] + environment(phi_ref, psi_ref, chip_pairs(layout.local_bits[0], far)))


def other_line_kernel(layout, section, gates_ref, phi_ref, next_in, next_ref):
    _, chips = layout.place_of(lax.axis_index("long"))
    gate = gate_matrix(gates_ref, section)
    for pair in line_pairs(layout, layout.local_bits[section], 1 - (chips[0] & 1)):
        apply_at(gate, phi_ref, next_ref, pair)


def last_adjoint_kernel(layout, gates_ref, phi_ref, next_ref, own_ref, sent_ref):
    core, chips = layout.place_of(lax.axis_index("long"))
    gate = gate_matrix(gates_ref, SECTIONS - 1)
    for pair in all_pairs(layout, layout.local_bits[SECTIONS - 1]):
        apply_at(gate, phi_ref, next_ref, pair)
    for slot, out in enumerate((own_ref, sent_ref)):
        out[...] = joined(next_ref, chips[0] * 2 + (slot ^ core))


def last_pair(layout, d):
    bit = layout.local_bits[SECTIONS - 1]
    first = d & ~(1 << bit)
    return first, first + (1 << bit)


def insert_bits(rest, bits):
    for bit in sorted(bits):
        rest = (rest >> bit << bit + 1) + (rest & (1 << bit) - 1)
    return rest


def load_quad(ref, rest, bits, plane):
    d = insert_bits(rest, bits)
    quad = [d + (t1 << bits[0]) + (t0 << bits[1]) for t1 in range(2) for t0 in range(2)]
    return [jnp.concatenate([ref[k, q, plane] for q in quad], 0) for k in range(2)]


def section_kernel(layout, section, e0_ref, e1_ref, phi_ref, psi_ref, gate_ref, e_ref, joint, left):
    bits = layout.local_bits[section + 1], layout.local_bits[section]
    rests = psi_ref.shape[1] // 4
    q = joint.shape[0] // 2
    c = q // 4
    units = [(rest, u) for rest in range(rests) for u in range(2)]
    gaps = 2 * NS_ITERS - 2

    def add(rest, u):
        planes = [load_quad(phi_ref, rest, bits, p) for p in range(2)]
        term = dot3([jnp.concatenate(v, 0) for v in zip(*planes)], load_quad(psi_ref, rest, bits, u), NT)
        at = (slice(None), slice(u * q, u * q + q))
        joint[at] = term if rest == 0 else joint[at] + term

    def arrange(p):
        real = joint[:q, :q] + joint[q:, q:] if p == 0 else joint[q:, :q] - joint[:q, q:]
        for k, v in enumerate(split(real)):
            for u1 in range(2):
                for t1 in range(2):
                    for t0 in range(2):
                        rows = slice((u1 * 2 + t1) * c, (u1 * 2 + t1 + 1) * c)
                        lanes = slice((p * 2 + t0) * 2 * c, (p * 2 + t0 + 1) * 2 * c)
                        left[k, rows, lanes] = v[(t1 * 2 + t0) * c : (t1 * 2 + t0 + 1) * c, u1 * 2 * c : (u1 + 1) * 2 * c]

    def beside(gap):
        for unit in units[gap * len(units) // gaps : (gap + 1) * len(units) // gaps] if gap < gaps else ():
            add(*unit)
        if gap >= gaps:
            arrange(gap - gaps)

    x = polar(e0_ref[...] + e1_ref[...], beside)
    right = []
    for v in split(x):
        r0, r1, i0, i1 = v[:c, : 2 * c], v[c:, : 2 * c], v[:c, 2 * c :], v[c:, 2 * c :]
        right.append(
            jnp.concatenate([jnp.concatenate([r0, r1, i0, i1], 1), jnp.concatenate([-i0, -i1, r0, r1], 1)], 0)
        )
    out = dot3((left[0], left[1]), right, NT)
    first, second = out[: 2 * c], out[2 * c :]
    e_ref[...] = jnp.concatenate([first[:, :c], second[:, :c], first[:, c:], second[:, c:]], 1)
    gate_ref[0], gate_ref[1] = split(as_matrix(x))


def apply_kernel(layout, section, gate_ref, psi_ref, next_ref):
    gate = gate_ref[0], gate_ref[1]
    for pair in all_pairs(layout, layout.local_bits[section]):
        apply_at(gate, psi_ref, next_ref, pair)


def ends_kernel(layout, gate_ref, psi_ref, own_ref, sent_ref):
    core, chips = layout.place_of(lax.axis_index("long"))
    gate = gate_ref[0], gate_ref[1]
    n = own_ref.shape[2]
    for t, first in enumerate(last_pair(layout, chips[0] * 2)):
        y = dot3(gate, load_pair(psi_ref, (first, first + 1)), NN)
        for plane in range(2):
            low, high = y[2 * plane * n : (2 * plane + 1) * n], y[(2 * plane + 1) * n : (2 * plane + 2) * n]
            own_ref[t, plane] = jnp.where(core == 0, low, high)
            sent_ref[t, plane] = jnp.where(core == 0, high, low)


def last_polar_kernel(e0_ref, e1_ref, adjoint_ref, gate_ref, out_ref, sem):
    copy = pltpu.make_async_copy(adjoint_ref, out_ref, sem)
    copy.start()
    gate_ref[...] = as_matrix(polar(e0_ref[...] + e1_ref[...]))
    copy.wait()


def unpack_kernel(layout, own_ref, got_ref, out_ref):
    core, _ = layout.place_of(lax.axis_index("long"))
    for plane in range(2):
        out_ref[plane] = unpacked(core, own_ref[plane], got_ref[plane])


def last_apply_kernel(layout, gate_ref, psi_own, psi_got, out_ref, state, sems):
    core, chips = layout.place_of(lax.axis_index("long"))
    t = chips[0] * 2 + core >> layout.local_bits[SECTIONS - 1] & 1
    n = psi_own.shape[2]
    inputs = [split(jnp.concatenate([psi[0, 0], psi[1, 0], psi[0, 1], psi[1, 1]], 0)) for psi in (psi_own, psi_got)]
    copies = []
    for plane in range(2):
        gate = split(gate_ref[pl.ds(pl.multiple_of((plane * 2 + t) * n, n), n)])
        state[plane] = unpacked(core, *[dot3(gate, x, NN) for x in inputs])
        copies.append(pltpu.make_async_copy(state.at[plane], out_ref.at[plane], sems.at[plane]))
        copies[plane].start()
    for copy in copies:
        copy.wait()


def call(kernel, name, outs, ins, flops, scratch=(), aliases=None, out_spaces={}):
    sizes = [int(np.prod(a.shape)) * a.dtype.itemsize for a in list(ins) + list(outs)]
    spec = pl.BlockSpec(memory_space=pltpu.VMEM)
    return pl.pallas_call(
        kernel,
        out_shape=outs,
        in_specs=[spec] * len(ins),
        out_specs=[pl.BlockSpec(memory_space=out_spaces.get(k, pltpu.VMEM)) for k in range(len(outs))],
        scratch_shapes=list(scratch),
        input_output_aliases=aliases or {},
        compiler_params=pltpu.CompilerParams(vmem_limit_bytes=VMEM_LIMIT),
        cost_estimate=pl.CostEstimate(flops=flops, bytes_accessed=sum(sizes), transcendentals=0),
        name=name,
    )(*ins)


def shards(initial_state, adjoint_state, current_gates):
    layout = Layout(lax.axis_size("long"))
    core_flip = layout.flip(layout.gate_bits[0])
    rows, lanes = initial_state.shape[1:]
    c = lanes // 2
    devices = layout.chips * 2
    whole = jax.ShapeDtypeStruct(initial_state.shape, F32)
    slab = jax.ShapeDtypeStruct((2, c, rows), F32)
    two_slabs = jax.ShapeDtypeStruct((2, 2, c, rows), F32)
    pieces = jax.ShapeDtypeStruct((2, devices, 2, c, rows), BF16)
    env = jax.ShapeDtypeStruct((lanes, 2 * lanes), F32)
    square = jax.ShapeDtypeStruct((2 * lanes, 2 * lanes), F32)
    apply_flops = 3 * 2 * (2 * lanes) ** 2 * (devices // 2) * rows

    def kernel(body, *args):
        return functools.partial(body, layout, *args)

    def both(e):
        for bit in layout.other_bits:
            e = e + lax.ppermute(e, "long", layout.flip(bit))
        return e, lax.ppermute(e, "long", core_flip)

    def home(own, sent):
        return jnp.stack([own, lax.ppermute(sent, "long", core_flip)])

    def pack(state):
        return call(kernel(pack_kernel), "pack", [slab] * 2, [state], 0)

    def after(x, *others):
        return lax.optimization_barrier((x, *others))[0]

    phi_home = home(*pack(adjoint_state))
    psi_own, psi_sent = pack(initial_state)
    phi_home, psi_own, psi_sent = lax.optimization_barrier((phi_home, psi_own, psi_sent))
    phi_near, phi_tail = gather_ring(phi_home, layout)
    phis = [call(kernel(first_gate_kernel), "first_gate", [pieces], [current_gates] + phi_near, apply_flops)[0]]
    phi_far = last_step(phi_tail, layout)
    phis += call(kernel(line_kernel), "line", [pieces] * 2, [current_gates, phis[0]], apply_flops)
    psi_near, psi_tail = gather_ring(home(psi_own, psi_sent), layout)
    psi_far = last_step([psi_tail[0], after(psi_tail[1], phis[1])], layout)
    ins = [current_gates] + psi_near + phi_far + [phis[0]]
    phis[0], psi, total = call(
        kernel(near_kernel), "near", [pieces, pieces, square], ins, apply_flops, aliases={len(ins) - 1: 0}
    )

    def other_line(section):
        ins = [current_gates, phis[section - 1], phis[section]]
        return call(
            kernel(other_line_kernel, section), "other_line", [pieces], ins, apply_flops // 2, aliases={2: 0}
        )[0]

    phis[1] = other_line(1)
    phis[2] = other_line(2)
    total = after(total, phis[2])
    psi, e = call(
        kernel(far_kernel), "far", [pieces, env], psi_far + [total, phis[0], psi], apply_flops // 4, aliases={4: 0}
    )
    gate_pair = jax.ShapeDtypeStruct((2,) + square.shape, BF16)
    for section in range(SECTIONS - 1):
        e0, e1 = both(e)
        if section == 0:
            phi, phi_own, phi_sent = call(
                kernel(last_adjoint_kernel),
                "last_adjoint",
                [pieces, slab, slab],
                [current_gates, phis[2]],
                apply_flops,
            )
            phis.append(phi)
            psi = after(psi, phi)
        else:
            (psi,) = call(kernel(apply_kernel, section - 1), "apply", [pieces], [gate, psi], apply_flops)
        if section == 1:
            phi_got = lax.ppermute(after(phi_sent, e), "long", core_flip)
        gate, e = call(
            kernel(section_kernel, section),
            "section",
            [gate_pair, env],
            [e0, e1, phis[section + 1], psi],
            4 * apply_flops,
            [pltpu.VMEM((4 * lanes, 4 * lanes), F32), pltpu.VMEM((2, 2 * lanes, 4 * lanes), BF16)],
        )
    e0, e1 = both(e)
    psi_own, psi_sent = call(kernel(ends_kernel), "ends", [two_slabs, two_slabs], [gate, psi], apply_flops // 4)
    psi_got = lax.ppermute(psi_sent, "long", core_flip)
    (adjoint,) = call(kernel(unpack_kernel), "unpack", [whole], [after(phi_own, e), phi_got], 0)
    gate, final_adjoint = call(
        last_polar_kernel,
        "last_polar",
        [square, whole],
        [e0, e1, adjoint],
        2 * apply_flops,
        [pltpu.SemaphoreType.DMA],
        out_spaces={1: pl.ANY},
    )
    (final_state,) = call(
        kernel(last_apply_kernel),
        "last_apply",
        [whole],
        [gate, psi_own, psi_got],
        apply_flops // 4,
        [pltpu.VMEM(initial_state.shape, F32), pltpu.SemaphoreType.DMA((2,))],
        out_spaces={0: pl.ANY},
    )
    return final_state, final_adjoint


def solution(mesh):
    return jax.shard_map(
        shards,
        mesh=mesh,
        in_specs=(
            P(None, ("groups", "long"), None),
            P(None, ("groups", "long"), None),
            P("groups", None, None, None),
        ),
        out_specs=(P(None, ("groups", "long"), None), P(None, ("groups", "long"), None)),
        check_vma=False,
    )
```

```python
import functools

import jax
import jax.numpy as jnp
import numpy as np
from jax import lax
from jax.experimental import pallas as pl
from jax.experimental.pallas import tpu as pltpu
from jax.sharding import PartitionSpec as P

SECTIONS = 4
NS_ITERS = 8

F32, BF16 = jnp.float32, jnp.bfloat16
NN = (((1,), (0,)), ((), ()))
NT = (((1,), (1,)), ((), ()))
VMEM_LIMIT = 24 * 2**20


class Layout:
    def __init__(self, size):
        bits = size.bit_length() - 1
        self.size = size
        self.partner_bits = [bits - 1, bits // 2, 0, 1]
        self.gate_bits = sorted(set(self.partner_bits))
        self.other_bits = [b for b in range(bits) if b not in self.gate_bits]
        self.local_bits = [self.gate_bits.index(b) for b in self.partner_bits]
        self.chips = 2 ** (len(self.gate_bits) - 1)

    def chip(self, index):
        return sum((index >> b & 1) << j for j, b in enumerate(self.gate_bits[1:]))

    def ring_position(self, chip):
        line, turn = chip >> 1, chip & 1
        return self.chips - 1 - line if turn else line

    def chip_at(self, position):
        position %= self.chips
        if position < self.chips // 2:
            return position << 1
        return (self.chips - 1 - position) << 1 | 1

    def shifted(self, index, step):
        chip = self.chip_at(self.ring_position(self.chip(index)) + step)
        for j, b in enumerate(self.gate_bits[1:]):
            index = index & ~(1 << b) | (chip >> j & 1) << b
        return index

    def ring(self, step):
        return [(i, self.shifted(i, step)) for i in range(self.size)]

    def flip(self, bit):
        return [(i, i ^ 1 << bit) for i in range(self.size)]

    def place_of(self, index):
        position = self.ring_position_traced(self.chip(index))
        half = self.chips // 2
        steps = [0] + [s for k in range(1, half) for s in (-k, k)] + [half]
        return index >> self.gate_bits[0] & 1, [self.chip_at_traced(position + s) for s in steps]

    def ring_position_traced(self, chip):
        line, turn = chip >> 1, chip & 1
        return jnp.where(turn == 1, self.chips - 1 - line, line)

    def chip_at_traced(self, position):
        position = position & self.chips - 1
        return jnp.where(position < self.chips // 2, position << 1, (self.chips - 1 - position) << 1 | 1)


STEPS = (1, -1)


def gather_ring(home, layout):
    blocks, ends = [home], [home, home]
    for _ in range(1, layout.chips // 2):
        ends = [lax.ppermute(end, "long", layout.ring(step)) for end, step in zip(ends, STEPS)]
        blocks += ends
    return blocks, [ends[0][:1], ends[1][1:]]


def last_step(tail, layout):
    return [lax.ppermute(end, "long", layout.ring(step)) for end, step in zip(tail, STEPS)]


def split(x):
    high = x.astype(BF16)
    return high, (x - high.astype(F32)).astype(BF16)


def dot(a, b, dims):
    return lax.dot_general(a, b, dims, preferred_element_type=F32)


def dot3(a, b, dims):
    return dot(a[0], b[0], dims) + (dot(a[0], b[1], dims) + dot(a[1], b[0], dims))


def turned(a):
    n = a.shape[1] // 2
    return jnp.concatenate([-a[:, n:], a[:, :n]], 1)


def as_matrix(a):
    n = a.shape[1] // 2
    return jnp.concatenate([jnp.concatenate([a[:, :n], -a[:, n:]], 1), jnp.concatenate([a[:, n:], a[:, :n]], 1)], 0)


def polar(e, beside=lambda gap: None):
    scale = lax.rsqrt(jnp.sum(e * e) + 1e-6)
    x = e
    n = x.shape[0]
    for k in range(NS_ITERS):
        xs = split(x)
        turns = [turned(v) for v in xs]
        beside(2 * k)
        h = jnp.concatenate([dot3(xs, xs, NT), dot3(xs, turns, NT)], 1)
        h = split(h * (scale * scale) if k == 0 else h)
        beside(2 * k + 1)
        rows = [jnp.concatenate(pair, 0) for pair in zip(xs, turns)]
        both = dot(jnp.concatenate(h, 0), rows[0], NN)
        x = 1.5 * x - 0.5 * (both[:n] + both[n:] + dot(h[0], rows[1], NN))
        x = x * scale if k == 0 else x
    return x


def load_pair(ref, pair):
    return [jnp.concatenate([ref[k, d, plane] for plane in range(2) for d in pair], 0) for k in range(2)]


def store_pair(ref, pair, y):
    n = y.shape[0] // 4
    for k, v in enumerate(split(y)):
        for plane in range(2):
            for t, d in enumerate(pair):
                ref[k, d, plane] = v[(2 * plane + t) * n : (2 * plane + t + 1) * n]


def apply_at(gate, source, target, pair):
    store_pair(target, pair, dot3(gate, load_pair(source, pair), NN))


def folded(total):
    n = total.shape[0] // 2
    return jnp.concatenate([total[:n, :n] + total[n:, n:], total[n:, :n] - total[:n, n:]], 1)


def environment(phi, psi, pairs):
    terms = [dot3(load_pair(phi, pair), load_pair(psi, pair), NT) for pair in pairs]
    return sum(terms[1:], terms[0])


def gate_matrix(gates_ref, section):
    return split(as_matrix(jnp.concatenate([gates_ref[section, 0], gates_ref[section, 1]], 1)))


def place(block, target, d):
    target[0, d], target[1, d] = split(block)


def joined(ref, d):
    return ref[0, d].astype(F32) + ref[1, d].astype(F32)


def unpacked(core, own, other):
    return jnp.concatenate([jnp.where(core == 0, own, other), jnp.where(core == 0, other, own)], 0).T


def pack_kernel(layout, x_ref, own_ref, sent_ref):
    core, _ = layout.place_of(lax.axis_index("long"))
    n = x_ref.shape[2] // 2
    for plane in range(2):
        t = x_ref[plane].T
        low, high = t[:n], t[n:]
        own_ref[plane] = jnp.where(core == 0, low, high)
        sent_ref[plane] = jnp.where(core == 0, high, low)


TURN = 1


def all_pairs(layout, bit):
    return [(d, d + (1 << bit)) for d in range(2 * layout.chips) if not d >> bit & 1]


def line_pairs(layout, bit, turn):
    return [tuple(d + (turn << TURN) for d in pair) for pair in all_pairs(layout, bit) if not pair[0] >> TURN & 1]


def chip_pairs(bit, chip):
    firsts = [(chip * 2 + slot) & ~(1 << bit) for slot in range(2)]
    return [(d, d + (1 << bit)) for d in firsts]


def near_pairs(layout, far):
    bit = layout.local_bits[0]
    others = [far ^ k for k in range(1, layout.chips) if not k >> bit - 1 & 1]
    return [pair for chip in others for pair in chip_pairs(bit, chip)]


def place_blocks(blocks, chips, core, target):
    for block, chip in zip(blocks, chips):
        for slot in range(2):
            place(block[slot], target, chip * 2 + (slot ^ core))


def place_far(halves, chip, core, target):
    for slot in range(2):
        place(halves[slot][0], target, chip * 2 + (slot ^ core))


def first_gate_kernel(layout, gates_ref, *refs):
    *blocks, phi_ref = refs
    core, chips = layout.place_of(lax.axis_index("long"))
    place_blocks(blocks, chips, core, phi_ref)
    gate = gate_matrix(gates_ref, 0)
    for pair in near_pairs(layout, chips[-1]):
        apply_at(gate, phi_ref, phi_ref, pair)


def line_kernel(layout, gates_ref, phi0_ref, phi1_ref, phi2_ref):
    _, chips = layout.place_of(lax.axis_index("long"))
    for s, source, target in ((1, phi0_ref, phi1_ref), (2, phi1_ref, phi2_ref)):
        gate = gate_matrix(gates_ref, s)
        for pair in line_pairs(layout, layout.local_bits[s], chips[0] & 1):
            apply_at(gate, source, target, pair)


def near_kernel(layout, *refs):
    *blocks, phi_ref, psi_ref, total_ref = refs
    core, chips = layout.place_of(lax.axis_index("long"))
    place_blocks(blocks, chips, core, psi_ref)
    total_ref[...] = environment(phi_ref, psi_ref, near_pairs(layout, chips[-1]))


def other_line_kernel(layout, gates_ref, far_a, far_b, phi0_in, phi1_in, phi2_in, phi0_ref, phi1_ref, phi2_ref):
    core, chips = layout.place_of(lax.axis_index("long"))
    place_far((far_a, far_b), chips[-1], core, phi0_ref)
    gate = gate_matrix(gates_ref, 0)
    for pair in chip_pairs(layout.local_bits[0], chips[-1]):
        apply_at(gate, phi0_ref, phi0_ref, pair)
    for s, source, target in ((1, phi0_ref, phi1_ref), (2, phi1_ref, phi2_ref)):
        gate = gate_matrix(gates_ref, s)
        for pair in line_pairs(layout, layout.local_bits[s], 1 - (chips[0] & 1)):
            apply_at(gate, source, target, pair)


def far_kernel(layout, psi_a, psi_b, total_ref, phi_ref, psi_in, psi_ref, e_ref):
    core, chips = layout.place_of(lax.axis_index("long"))
    far = chips[-1]
    place_far((psi_a, psi_b), far, core, psi_ref)
    e_ref[...] = folded(total_ref[...] + environment(phi_ref, psi_ref, chip_pairs(layout.local_bits[0], far)))


def last_adjoint_kernel(layout, gates_ref, phi_ref, next_ref, own_ref, sent_ref):
    core, chips = layout.place_of(lax.axis_index("long"))
    gate = gate_matrix(gates_ref, SECTIONS - 1)
    for pair in all_pairs(layout, layout.local_bits[SECTIONS - 1]):
        apply_at(gate, phi_ref, next_ref, pair)
    for slot, out in enumerate((own_ref, sent_ref)):
        out[...] = joined(next_ref, chips[0] * 2 + (slot ^ core))


def last_pair(layout, d):
    bit = layout.local_bits[SECTIONS - 1]
    first = d & ~(1 << bit)
    return first, first + (1 << bit)


def insert_bits(rest, bits):
    for bit in sorted(bits):
        rest = (rest >> bit << bit + 1) + (rest & (1 << bit) - 1)
    return rest


def load_quad(ref, rest, bits, plane):
    d = insert_bits(rest, bits)
    quad = [d + (t1 << bits[0]) + (t0 << bits[1]) for t1 in range(2) for t0 in range(2)]
    return [jnp.concatenate([ref[k, q, plane] for q in quad], 0) for k in range(2)]


def section_kernel(layout, section, e0_ref, e1_ref, phi_ref, psi_ref, gate_ref, e_ref, joint, left):
    bits = layout.local_bits[section + 1], layout.local_bits[section]
    rests = psi_ref.shape[1] // 4
    q = joint.shape[0] // 2
    c = q // 4
    units = [(rest, u) for rest in range(rests) for u in range(2)]
    gaps = 2 * NS_ITERS - 2

    def add(rest, u):
        planes = [load_quad(phi_ref, rest, bits, p) for p in range(2)]
        term = dot3([jnp.concatenate(v, 0) for v in zip(*planes)], load_quad(psi_ref, rest, bits, u), NT)
        at = (slice(None), slice(u * q, u * q + q))
        joint[at] = term if rest == 0 else joint[at] + term

    def arrange(p):
        real = joint[:q, :q] + joint[q:, q:] if p == 0 else joint[q:, :q] - joint[:q, q:]
        for k, v in enumerate(split(real)):
            for u1 in range(2):
                for t1 in range(2):
                    for t0 in range(2):
                        rows = slice((u1 * 2 + t1) * c, (u1 * 2 + t1 + 1) * c)
                        lanes = slice((p * 2 + t0) * 2 * c, (p * 2 + t0 + 1) * 2 * c)
                        left[k, rows, lanes] = v[(t1 * 2 + t0) * c : (t1 * 2 + t0 + 1) * c, u1 * 2 * c : (u1 + 1) * 2 * c]

    def beside(gap):
        for unit in units[gap * len(units) // gaps : (gap + 1) * len(units) // gaps] if gap < gaps else ():
            add(*unit)
        if gap >= gaps:
            arrange(gap - gaps)

    x = polar(e0_ref[...] + e1_ref[...], beside)
    right = []
    for v in split(x):
        r0, r1, i0, i1 = v[:c, : 2 * c], v[c:, : 2 * c], v[:c, 2 * c :], v[c:, 2 * c :]
        right.append(
            jnp.concatenate([jnp.concatenate([r0, r1, i0, i1], 1), jnp.concatenate([-i0, -i1, r0, r1], 1)], 0)
        )
    out = dot3((left[0], left[1]), right, NT)
    first, second = out[: 2 * c], out[2 * c :]
    e_ref[...] = jnp.concatenate([first[:, :c], second[:, :c], first[:, c:], second[:, c:]], 1)
    gate_ref[0], gate_ref[1] = split(as_matrix(x))


def apply_kernel(layout, section, gate_ref, psi_ref, next_ref):
    gate = gate_ref[0], gate_ref[1]
    for pair in all_pairs(layout, layout.local_bits[section]):
        apply_at(gate, psi_ref, next_ref, pair)


def ends_kernel(layout, gate_ref, psi_ref, own_ref, sent_ref):
    core, chips = layout.place_of(lax.axis_index("long"))
    gate = gate_ref[0], gate_ref[1]
    n = own_ref.shape[2]
    for t, first in enumerate(last_pair(layout, chips[0] * 2)):
        y = dot3(gate, load_pair(psi_ref, (first, first + 1)), NN)
        for plane in range(2):
            low, high = y[2 * plane * n : (2 * plane + 1) * n], y[(2 * plane + 1) * n : (2 * plane + 2) * n]
            own_ref[t, plane] = jnp.where(core == 0, low, high)
            sent_ref[t, plane] = jnp.where(core == 0, high, low)


def last_polar_kernel(e0_ref, e1_ref, adjoint_ref, gate_ref, out_ref, sem):
    copy = pltpu.make_async_copy(adjoint_ref, out_ref, sem)
    copy.start()
    gate_ref[...] = as_matrix(polar(e0_ref[...] + e1_ref[...]))
    copy.wait()


def unpack_kernel(layout, own_ref, got_ref, out_ref):
    core, _ = layout.place_of(lax.axis_index("long"))
    for plane in range(2):
        out_ref[plane] = unpacked(core, own_ref[plane], got_ref[plane])


def last_apply_kernel(layout, gate_ref, psi_own, psi_got, out_ref, state, sems):
    core, chips = layout.place_of(lax.axis_index("long"))
    t = chips[0] * 2 + core >> layout.local_bits[SECTIONS - 1] & 1
    n = psi_own.shape[2]
    gate = split(jnp.concatenate([gate_ref[pl.ds(pl.multiple_of((plane * 2 + t) * n, n), n)] for plane in range(2)], 0))
    halves = [
        dot3(gate, split(jnp.concatenate([psi[0, 0], psi[1, 0], psi[0, 1], psi[1, 1]], 0)), NN)
        for psi in (psi_own, psi_got)
    ]
    copies = []
    for plane in range(2):
        state[plane] = unpacked(core, *[y[plane * n : (plane + 1) * n] for y in halves])
        copies.append(pltpu.make_async_copy(state.at[plane], out_ref.at[plane], sems.at[plane]))
        copies[plane].start()
    for copy in copies:
        copy.wait()


def call(kernel, name, outs, ins, flops, scratch=(), aliases=None, out_spaces={}):
    sizes = [int(np.prod(a.shape)) * a.dtype.itemsize for a in list(ins) + list(outs)]
    spec = pl.BlockSpec(memory_space=pltpu.VMEM)
    return pl.pallas_call(
        kernel,
        out_shape=outs,
        in_specs=[spec] * len(ins),
        out_specs=[pl.BlockSpec(memory_space=out_spaces.get(k, pltpu.VMEM)) for k in range(len(outs))],
        scratch_shapes=list(scratch),
        input_output_aliases=aliases or {},
        compiler_params=pltpu.CompilerParams(vmem_limit_bytes=VMEM_LIMIT),
        cost_estimate=pl.CostEstimate(flops=flops, bytes_accessed=sum(sizes), transcendentals=0),
        name=name,
    )(*ins)


def shards(initial_state, adjoint_state, current_gates):
    layout = Layout(lax.axis_size("long"))
    core_flip = layout.flip(layout.gate_bits[0])
    rows, lanes = initial_state.shape[1:]
    c = lanes // 2
    devices = layout.chips * 2
    whole = jax.ShapeDtypeStruct(initial_state.shape, F32)
    slab = jax.ShapeDtypeStruct((2, c, rows), F32)
    two_slabs = jax.ShapeDtypeStruct((2, 2, c, rows), F32)
    pieces = jax.ShapeDtypeStruct((2, devices, 2, c, rows), BF16)
    env = jax.ShapeDtypeStruct((lanes, 2 * lanes), F32)
    square = jax.ShapeDtypeStruct((2 * lanes, 2 * lanes), F32)
    apply_flops = 3 * 2 * (2 * lanes) ** 2 * (devices // 2) * rows

    def kernel(body, *args):
        return functools.partial(body, layout, *args)

    def both(e):
        for bit in layout.other_bits:
            e = e + lax.ppermute(e, "long", layout.flip(bit))
        return e, lax.ppermute(e, "long", core_flip)

    def home(own, sent):
        return jnp.stack([own, lax.ppermute(sent, "long", core_flip)])

    def pack(state):
        return call(kernel(pack_kernel), "pack", [slab] * 2, [state], 0)

    def after(x, *others):
        return lax.optimization_barrier((x, *others))[0]

    phi_home = home(*pack(adjoint_state))
    psi_own, psi_sent = pack(initial_state)
    phi_home, psi_own, psi_sent = lax.optimization_barrier((phi_home, psi_own, psi_sent))
    phi_near, phi_tail = gather_ring(phi_home, layout)
    phis = [call(kernel(first_gate_kernel), "first_gate", [pieces], [current_gates] + phi_near, apply_flops)[0]]
    phi_far = last_step(phi_tail, layout)
    phis += call(kernel(line_kernel), "line", [pieces] * 2, [current_gates, phis[0]], apply_flops)
    psi_near, psi_tail = gather_ring(home(psi_own, psi_sent), layout)
    psi_far = last_step([psi_tail[0], after(psi_tail[1], phis[1])], layout)
    psi, total = call(kernel(near_kernel), "near", [pieces, square], psi_near + [phis[0]], 3 * apply_flops // 4)
    phis = list(
        call(
            kernel(other_line_kernel),
            "other_line",
            [pieces] * 3,
            [current_gates] + phi_far + phis,
            5 * apply_flops // 4,
            aliases={3: 0, 4: 1, 5: 2},
        )
    )
    total = after(total, phis[2])
    psi, e = call(
        kernel(far_kernel), "far", [pieces, env], psi_far + [total, phis[0], psi], apply_flops // 4, aliases={4: 0}
    )
    gate_pair = jax.ShapeDtypeStruct((2,) + square.shape, BF16)
    for section in range(SECTIONS - 1):
        e0, e1 = both(e)
        if section == 0:
            phi, phi_own, phi_sent = call(
                kernel(last_adjoint_kernel),
                "last_adjoint",
                [pieces, slab, slab],
                [current_gates, phis[2]],
                apply_flops,
            )
            phis.append(phi)
            psi = after(psi, phi)
        else:
            (psi,) = call(kernel(apply_kernel, section - 1), "apply", [pieces], [gate, psi], apply_flops)
        if section == 1:
            phi_got = lax.ppermute(after(phi_sent, e), "long", core_flip)
        gate, e = call(
            kernel(section_kernel, section),
            "section",
            [gate_pair, env],
            [e0, e1, phis[section + 1], psi],
            4 * apply_flops,
            [pltpu.VMEM((4 * lanes, 4 * lanes), F32), pltpu.VMEM((2, 2 * lanes, 4 * lanes), BF16)],
        )
    e0, e1 = both(e)
    psi_own, psi_sent = call(kernel(ends_kernel), "ends", [two_slabs, two_slabs], [gate, psi], apply_flops // 4)
    psi_got = lax.ppermute(psi_sent, "long", core_flip)
    (adjoint,) = call(kernel(unpack_kernel), "unpack", [whole], [after(phi_own, e), phi_got], 0)
    gate, final_adjoint = call(
        last_polar_kernel,
        "last_polar",
        [square, whole],
        [e0, e1, adjoint],
        2 * apply_flops,
        [pltpu.SemaphoreType.DMA],
        out_spaces={1: pl.ANY},
    )
    (final_state,) = call(
        kernel(last_apply_kernel),
        "last_apply",
        [whole],
        [gate, psi_own, psi_got],
        apply_flops // 4,
        [pltpu.VMEM(initial_state.shape, F32), pltpu.SemaphoreType.DMA((2,))],
        out_spaces={0: pl.ANY},
    )
    return final_state, final_adjoint


def solution(mesh):
    return jax.shard_map(
        shards,
        mesh=mesh,
        in_specs=(
            P(None, ("groups", "long"), None),
            P(None, ("groups", "long"), None),
            P("groups", None, None, None),
        ),
        out_specs=(P(None, ("groups", "long"), None), P(None, ("groups", "long"), None)),
        check_vma=False,
    )
```

```python
import functools

import jax
import jax.numpy as jnp
import numpy as np
from jax import lax
from jax.experimental import pallas as pl
from jax.experimental.pallas import tpu as pltpu
from jax.sharding import PartitionSpec as P

SECTIONS = 4
NS_ITERS = 8

F32, BF16 = jnp.float32, jnp.bfloat16
NN = (((1,), (0,)), ((), ()))
NT = (((1,), (1,)), ((), ()))
VMEM_LIMIT = 24 * 2**20


class Layout:
    def __init__(self, size):
        bits = size.bit_length() - 1
        self.size = size
        self.partner_bits = [bits - 1, bits // 2, 0, 1]
        self.gate_bits = sorted(set(self.partner_bits))
        self.other_bits = [b for b in range(bits) if b not in self.gate_bits]
        self.local_bits = [self.gate_bits.index(b) for b in self.partner_bits]
        self.chips = 2 ** (len(self.gate_bits) - 1)

    def chip(self, index):
        return sum((index >> b & 1) << j for j, b in enumerate(self.gate_bits[1:]))

    def ring_position(self, chip):
        line, turn = chip >> 1, chip & 1
        return self.chips - 1 - line if turn else line

    def chip_at(self, position):
        position %= self.chips
        if position < self.chips // 2:
            return position << 1
        return (self.chips - 1 - position) << 1 | 1

    def shifted(self, index, step):
        chip = self.chip_at(self.ring_position(self.chip(index)) + step)
        for j, b in enumerate(self.gate_bits[1:]):
            index = index & ~(1 << b) | (chip >> j & 1) << b
        return index

    def ring(self, step):
        return [(i, self.shifted(i, step)) for i in range(self.size)]

    def flip(self, bit):
        return [(i, i ^ 1 << bit) for i in range(self.size)]

    def place_of(self, index):
        position = self.ring_position_traced(self.chip(index))
        half = self.chips // 2
        steps = [0] + [s for k in range(1, half) for s in (-k, k)] + [half]
        return index >> self.gate_bits[0] & 1, [self.chip_at_traced(position + s) for s in steps]

    def ring_position_traced(self, chip):
        line, turn = chip >> 1, chip & 1
        return jnp.where(turn == 1, self.chips - 1 - line, line)

    def chip_at_traced(self, position):
        position = position & self.chips - 1
        return jnp.where(position < self.chips // 2, position << 1, (self.chips - 1 - position) << 1 | 1)


STEPS = (1, -1)


def gather_ring(home, layout):
    blocks, ends = [home], [home, home]
    for _ in range(1, layout.chips // 2):
        ends = [lax.ppermute(end, "long", layout.ring(step)) for end, step in zip(ends, STEPS)]
        blocks += ends
    return blocks, [ends[0][:1], ends[1][1:]]


def last_step(tail, layout):
    return [lax.ppermute(end, "long", layout.ring(step)) for end, step in zip(tail, STEPS)]


def split(x):
    high = x.astype(BF16)
    return high, (x - high.astype(F32)).astype(BF16)


def dot(a, b, dims):
    return lax.dot_general(a, b, dims, preferred_element_type=F32)


def dot3(a, b, dims):
    return dot(a[0], b[0], dims) + (dot(a[0], b[1], dims) + dot(a[1], b[0], dims))


def turned(a):
    n = a.shape[1] // 2
    return jnp.concatenate([-a[:, n:], a[:, :n]], 1)


def as_matrix(a):
    n = a.shape[1] // 2
    return jnp.concatenate([jnp.concatenate([a[:, :n], -a[:, n:]], 1), jnp.concatenate([a[:, n:], a[:, :n]], 1)], 0)


def polar(e, beside=lambda gap: None):
    scale = lax.rsqrt(jnp.sum(e * e) + 1e-6)
    x = e
    n = x.shape[0]
    for k in range(NS_ITERS):
        xs = split(x)
        turns = [turned(v) for v in xs]
        beside(2 * k)
        h = jnp.concatenate([dot3(xs, xs, NT), dot3(xs, turns, NT)], 1)
        h = split(h * (scale * scale) if k == 0 else h)
        beside(2 * k + 1)
        rows = [jnp.concatenate(pair, 0) for pair in zip(xs, turns)]
        both = dot(jnp.concatenate(h, 0), rows[0], NN)
        x = 1.5 * x - 0.5 * (both[:n] + both[n:] + dot(h[0], rows[1], NN))
        x = x * scale if k == 0 else x
    return x


def load_pair(ref, pair):
    return [jnp.concatenate([ref[k, d, plane] for plane in range(2) for d in pair], 0) for k in range(2)]


def store_pair(ref, pair, y):
    n = y.shape[0] // 4
    for k, v in enumerate(split(y)):
        for plane in range(2):
            for t, d in enumerate(pair):
                ref[k, d, plane] = v[(2 * plane + t) * n : (2 * plane + t + 1) * n]


def apply_at(gate, source, target, pair):
    store_pair(target, pair, dot3(gate, load_pair(source, pair), NN))


def folded(total):
    n = total.shape[0] // 2
    return jnp.concatenate([total[:n, :n] + total[n:, n:], total[n:, :n] - total[:n, n:]], 1)


def environment(phi, psi, pairs):
    terms = [dot3(load_pair(phi, pair), load_pair(psi, pair), NT) for pair in pairs]
    return sum(terms[1:], terms[0])


def gate_matrix(gates_ref, section):
    return split(as_matrix(jnp.concatenate([gates_ref[section, 0], gates_ref[section, 1]], 1)))


def place(block, target, d):
    target[0, d], target[1, d] = split(block)


def joined(ref, d):
    return ref[0, d].astype(F32) + ref[1, d].astype(F32)


def unpacked(core, own, other):
    return jnp.concatenate([jnp.where(core == 0, own, other), jnp.where(core == 0, other, own)], 0).T


def pack_kernel(layout, x_ref, own_ref, sent_ref):
    core, _ = layout.place_of(lax.axis_index("long"))
    n = x_ref.shape[2] // 2
    for plane in range(2):
        t = x_ref[plane].T
        low, high = t[:n], t[n:]
        own_ref[plane] = jnp.where(core == 0, low, high)
        sent_ref[plane] = jnp.where(core == 0, high, low)


TURN = 1


def all_pairs(layout, bit):
    return [(d, d + (1 << bit)) for d in range(2 * layout.chips) if not d >> bit & 1]


def line_pairs(layout, bit, turn):
    return [tuple(d + (turn << TURN) for d in pair) for pair in all_pairs(layout, bit) if not pair[0] >> TURN & 1]


def chip_pairs(bit, chip):
    firsts = [(chip * 2 + slot) & ~(1 << bit) for slot in range(2)]
    return [(d, d + (1 << bit)) for d in firsts]


def near_pairs(layout, far):
    bit = layout.local_bits[0]
    others = [far ^ k for k in range(1, layout.chips) if not k >> bit - 1 & 1]
    return [pair for chip in others for pair in chip_pairs(bit, chip)]


def place_blocks(blocks, chips, core, target):
    for block, chip in zip(blocks, chips):
        for slot in range(2):
            place(block[slot], target, chip * 2 + (slot ^ core))


def place_far(halves, chip, core, target):
    for slot in range(2):
        place(halves[slot][0], target, chip * 2 + (slot ^ core))


def first_gate_kernel(layout, gates_ref, *refs):
    *blocks, phi_ref = refs
    core, chips = layout.place_of(lax.axis_index("long"))
    place_blocks(blocks, chips, core, phi_ref)
    gate = gate_matrix(gates_ref, 0)
    for pair in near_pairs(layout, chips[-1]):
        apply_at(gate, phi_ref, phi_ref, pair)


def line_kernel(layout, gates_ref, phi0_ref, phi1_ref, phi2_ref):
    _, chips = layout.place_of(lax.axis_index("long"))
    for s, source, target in ((1, phi0_ref, phi1_ref), (2, phi1_ref, phi2_ref)):
        gate = gate_matrix(gates_ref, s)
        for pair in line_pairs(layout, layout.local_bits[s], chips[0] & 1):
            apply_at(gate, source, target, pair)


def near_kernel(layout, *refs):
    *blocks, phi_ref, psi_ref, total_ref = refs
    core, chips = layout.place_of(lax.axis_index("long"))
    place_blocks(blocks, chips, core, psi_ref)
    total_ref[...] = environment(phi_ref, psi_ref, near_pairs(layout, chips[-1]))


def other_line_kernel(layout, gates_ref, far_a, far_b, phi0_in, phi1_in, phi2_in, phi0_ref, phi1_ref, phi2_ref):
    core, chips = layout.place_of(lax.axis_index("long"))
    place_far((far_a, far_b), chips[-1], core, phi0_ref)
    gate = gate_matrix(gates_ref, 0)
    for pair in chip_pairs(layout.local_bits[0], chips[-1]):
        apply_at(gate, phi0_ref, phi0_ref, pair)
    for s, source, target in ((1, phi0_ref, phi1_ref), (2, phi1_ref, phi2_ref)):
        gate = gate_matrix(gates_ref, s)
        for pair in line_pairs(layout, layout.local_bits[s], 1 - (chips[0] & 1)):
            apply_at(gate, source, target, pair)


def far_kernel(layout, psi_a, psi_b, total_ref, phi_ref, psi_in, psi_ref, e_ref):
    core, chips = layout.place_of(lax.axis_index("long"))
    far = chips[-1]
    place_far((psi_a, psi_b), far, core, psi_ref)
    e_ref[...] = folded(total_ref[...] + environment(phi_ref, psi_ref, chip_pairs(layout.local_bits[0], far)))


def last_adjoint_kernel(layout, gates_ref, phi_ref, next_ref, own_ref, sent_ref):
    core, chips = layout.place_of(lax.axis_index("long"))
    gate = gate_matrix(gates_ref, SECTIONS - 1)
    for pair in all_pairs(layout, layout.local_bits[SECTIONS - 1]):
        apply_at(gate, phi_ref, next_ref, pair)
    for slot, out in enumerate((own_ref, sent_ref)):
        out[...] = joined(next_ref, chips[0] * 2 + (slot ^ core))


def last_pair(layout, d):
    bit = layout.local_bits[SECTIONS - 1]
    first = d & ~(1 << bit)
    return first, first + (1 << bit)


def insert_bits(rest, bits):
    for bit in sorted(bits):
        rest = (rest >> bit << bit + 1) + (rest & (1 << bit) - 1)
    return rest


def load_quad(ref, rest, bits, plane):
    d = insert_bits(rest, bits)
    quad = [d + (t1 << bits[0]) + (t0 << bits[1]) for t1 in range(2) for t0 in range(2)]
    return [jnp.concatenate([ref[k, q, plane] for q in quad], 0) for k in range(2)]


def section_kernel(layout, section, e0_ref, e1_ref, phi_ref, psi_ref, gate_ref, e_ref, joint, left):
    bits = layout.local_bits[section + 1], layout.local_bits[section]
    rests = psi_ref.shape[1] // 4
    q = joint.shape[0] // 2
    c = q // 4
    units = [(rest, u) for rest in range(rests) for u in range(2)]
    gaps = 2 * NS_ITERS - 2

    def add(rest, u):
        planes = [load_quad(phi_ref, rest, bits, p) for p in range(2)]
        term = dot3([jnp.concatenate(v, 0) for v in zip(*planes)], load_quad(psi_ref, rest, bits, u), NT)
        at = (slice(None), slice(u * q, u * q + q))
        joint[at] = term if rest == 0 else joint[at] + term

    def arrange(p):
        real = joint[:q, :q] + joint[q:, q:] if p == 0 else joint[q:, :q] - joint[:q, q:]
        for k, v in enumerate(split(real)):
            for u1 in range(2):
                for t1 in range(2):
                    for t0 in range(2):
                        rows = slice((u1 * 2 + t1) * c, (u1 * 2 + t1 + 1) * c)
                        lanes = slice((p * 2 + t0) * 2 * c, (p * 2 + t0 + 1) * 2 * c)
                        left[k, rows, lanes] = v[(t1 * 2 + t0) * c : (t1 * 2 + t0 + 1) * c, u1 * 2 * c : (u1 + 1) * 2 * c]

    def beside(gap):
        for unit in units[gap * len(units) // gaps : (gap + 1) * len(units) // gaps] if gap < gaps else ():
            add(*unit)
        if gap >= gaps:
            arrange(gap - gaps)

    x = polar(e0_ref[...] + e1_ref[...], beside)
    right = []
    for v in split(x):
        r0, r1, i0, i1 = v[:c, : 2 * c], v[c:, : 2 * c], v[:c, 2 * c :], v[c:, 2 * c :]
        right.append(
            jnp.concatenate([jnp.concatenate([r0, r1, i0, i1], 1), jnp.concatenate([-i0, -i1, r0, r1], 1)], 0)
        )
    two = dot(left[0], jnp.concatenate(right, 0), NT)
    out = two[:, : 2 * c] + two[:, 2 * c :] + dot(left[1], right[0], NT)
    first, second = out[: 2 * c], out[2 * c :]
    e_ref[...] = jnp.concatenate([first[:, :c], second[:, :c], first[:, c:], second[:, c:]], 1)
    gate_ref[0], gate_ref[1] = split(as_matrix(x))


def apply_kernel(layout, section, gate_ref, psi_ref, next_ref):
    gate = gate_ref[0], gate_ref[1]
    for pair in all_pairs(layout, layout.local_bits[section]):
        apply_at(gate, psi_ref, next_ref, pair)


def ends_kernel(layout, gate_ref, psi_ref, own_ref, sent_ref):
    core, chips = layout.place_of(lax.axis_index("long"))
    gate = gate_ref[0], gate_ref[1]
    n = own_ref.shape[2]
    for t, first in enumerate(last_pair(layout, chips[0] * 2)):
        y = dot3(gate, load_pair(psi_ref, (first, first + 1)), NN)
        for plane in range(2):
            low, high = y[2 * plane * n : (2 * plane + 1) * n], y[(2 * plane + 1) * n : (2 * plane + 2) * n]
            own_ref[t, plane] = jnp.where(core == 0, low, high)
            sent_ref[t, plane] = jnp.where(core == 0, high, low)


def last_polar_kernel(e0_ref, e1_ref, adjoint_ref, gate_ref, out_ref, sem):
    copy = pltpu.make_async_copy(adjoint_ref, out_ref, sem)
    copy.start()
    gate_ref[...] = as_matrix(polar(e0_ref[...] + e1_ref[...]))
    copy.wait()


def unpack_kernel(layout, own_ref, got_ref, out_ref):
    core, _ = layout.place_of(lax.axis_index("long"))
    for plane in range(2):
        out_ref[plane] = unpacked(core, own_ref[plane], got_ref[plane])


def last_apply_kernel(layout, gate_ref, psi_own, psi_got, out_ref, state, sems):
    core, chips = layout.place_of(lax.axis_index("long"))
    t = chips[0] * 2 + core >> layout.local_bits[SECTIONS - 1] & 1
    n = psi_own.shape[2]
    gate = split(jnp.concatenate([gate_ref[pl.ds(pl.multiple_of((plane * 2 + t) * n, n), n)] for plane in range(2)], 0))
    halves = [
        dot3(gate, split(jnp.concatenate([psi[0, 0], psi[1, 0], psi[0, 1], psi[1, 1]], 0)), NN)
        for psi in (psi_own, psi_got)
    ]
    copies = []
    for plane in range(2):
        state[plane] = unpacked(core, *[y[plane * n : (plane + 1) * n] for y in halves])
        copies.append(pltpu.make_async_copy(state.at[plane], out_ref.at[plane], sems.at[plane]))
        copies[plane].start()
    for copy in copies:
        copy.wait()


def call(kernel, name, outs, ins, flops, scratch=(), aliases=None, out_spaces={}):
    sizes = [int(np.prod(a.shape)) * a.dtype.itemsize for a in list(ins) + list(outs)]
    spec = pl.BlockSpec(memory_space=pltpu.VMEM)
    return pl.pallas_call(
        kernel,
        out_shape=outs,
        in_specs=[spec] * len(ins),
        out_specs=[pl.BlockSpec(memory_space=out_spaces.get(k, pltpu.VMEM)) for k in range(len(outs))],
        scratch_shapes=list(scratch),
        input_output_aliases=aliases or {},
        compiler_params=pltpu.CompilerParams(vmem_limit_bytes=VMEM_LIMIT),
        cost_estimate=pl.CostEstimate(flops=flops, bytes_accessed=sum(sizes), transcendentals=0),
        name=name,
    )(*ins)


def shards(initial_state, adjoint_state, current_gates):
    layout = Layout(lax.axis_size("long"))
    core_flip = layout.flip(layout.gate_bits[0])
    rows, lanes = initial_state.shape[1:]
    c = lanes // 2
    devices = layout.chips * 2
    whole = jax.ShapeDtypeStruct(initial_state.shape, F32)
    slab = jax.ShapeDtypeStruct((2, c, rows), F32)
    two_slabs = jax.ShapeDtypeStruct((2, 2, c, rows), F32)
    pieces = jax.ShapeDtypeStruct((2, devices, 2, c, rows), BF16)
    env = jax.ShapeDtypeStruct((lanes, 2 * lanes), F32)
    square = jax.ShapeDtypeStruct((2 * lanes, 2 * lanes), F32)
    apply_flops = 3 * 2 * (2 * lanes) ** 2 * (devices // 2) * rows

    def kernel(body, *args):
        return functools.partial(body, layout, *args)

    def both(e):
        for bit in layout.other_bits:
            e = e + lax.ppermute(e, "long", layout.flip(bit))
        return e, lax.ppermute(e, "long", core_flip)

    def home(own, sent):
        return jnp.stack([own, lax.ppermute(sent, "long", core_flip)])

    def pack(state):
        return call(kernel(pack_kernel), "pack", [slab] * 2, [state], 0)

    def after(x, *others):
        return lax.optimization_barrier((x, *others))[0]

    phi_home = home(*pack(adjoint_state))
    psi_own, psi_sent = pack(initial_state)
    phi_home, psi_own, psi_sent = lax.optimization_barrier((phi_home, psi_own, psi_sent))
    phi_near, phi_tail = gather_ring(phi_home, layout)
    phis = [call(kernel(first_gate_kernel), "first_gate", [pieces], [current_gates] + phi_near, apply_flops)[0]]
    phi_far = last_step(phi_tail, layout)
    phis += call(kernel(line_kernel), "line", [pieces] * 2, [current_gates, phis[0]], apply_flops)
    psi_near, psi_tail = gather_ring(home(psi_own, psi_sent), layout)
    psi_far = last_step([psi_tail[0], after(psi_tail[1], phis[1])], layout)
    psi, total = call(kernel(near_kernel), "near", [pieces, square], psi_near + [phis[0]], 3 * apply_flops // 4)
    phis = list(
        call(
            kernel(other_line_kernel),
            "other_line",
            [pieces] * 3,
            [current_gates] + phi_far + phis,
            5 * apply_flops // 4,
            aliases={3: 0, 4: 1, 5: 2},
        )
    )
    total = after(total, phis[2])
    psi, e = call(
        kernel(far_kernel), "far", [pieces, env], psi_far + [total, phis[0], psi], apply_flops // 4, aliases={4: 0}
    )
    gate_pair = jax.ShapeDtypeStruct((2,) + square.shape, BF16)
    for section in range(SECTIONS - 1):
        e0, e1 = both(e)
        if section == 0:
            phi, phi_own, phi_sent = call(
                kernel(last_adjoint_kernel),
                "last_adjoint",
                [pieces, slab, slab],
                [current_gates, phis[2]],
                apply_flops,
            )
            phis.append(phi)
            psi = after(psi, phi)
        else:
            (psi,) = call(kernel(apply_kernel, section - 1), "apply", [pieces], [gate, psi], apply_flops)
        if section == 1:
            phi_got = lax.ppermute(after(phi_sent, e), "long", core_flip)
        gate, e = call(
            kernel(section_kernel, section),
            "section",
            [gate_pair, env],
            [e0, e1, phis[section + 1], psi],
            4 * apply_flops,
            [pltpu.VMEM((4 * lanes, 4 * lanes), F32), pltpu.VMEM((2, 2 * lanes, 4 * lanes), BF16)],
        )
    e0, e1 = both(e)
    psi_own, psi_sent = call(kernel(ends_kernel), "ends", [two_slabs, two_slabs], [gate, psi], apply_flops // 4)
    psi_got = lax.ppermute(psi_sent, "long", core_flip)
    (adjoint,) = call(kernel(unpack_kernel), "unpack", [whole], [after(phi_own, e), phi_got], 0)
    gate, final_adjoint = call(
        last_polar_kernel,
        "last_polar",
        [square, whole],
        [e0, e1, adjoint],
        2 * apply_flops,
        [pltpu.SemaphoreType.DMA],
        out_spaces={1: pl.ANY},
    )
    (final_state,) = call(
        kernel(last_apply_kernel),
        "last_apply",
        [whole],
        [gate, psi_own, psi_got],
        apply_flops // 4,
        [pltpu.VMEM(initial_state.shape, F32), pltpu.SemaphoreType.DMA((2,))],
        out_spaces={0: pl.ANY},
    )
    return final_state, final_adjoint


def solution(mesh):
    return jax.shard_map(
        shards,
        mesh=mesh,
        in_specs=(
            P(None, ("groups", "long"), None),
            P(None, ("groups", "long"), None),
            P("groups", None, None, None),
        ),
        out_specs=(P(None, ("groups", "long"), None), P(None, ("groups", "long"), None)),
        check_vma=False,
    )
```

```python
import functools

import jax
import jax.numpy as jnp
import numpy as np
from jax import lax
from jax.experimental import pallas as pl
from jax.experimental.pallas import tpu as pltpu
from jax.sharding import PartitionSpec as P

SECTIONS = 4
NS_ITERS = 8

F32, BF16 = jnp.float32, jnp.bfloat16
NN = (((1,), (0,)), ((), ()))
NT = (((1,), (1,)), ((), ()))
VMEM_LIMIT = 24 * 2**20


class Layout:
    def __init__(self, size):
        bits = size.bit_length() - 1
        self.size = size
        self.partner_bits = [bits - 1, bits // 2, 0, 1]
        self.gate_bits = sorted(set(self.partner_bits))
        self.other_bits = [b for b in range(bits) if b not in self.gate_bits]
        self.local_bits = [self.gate_bits.index(b) for b in self.partner_bits]
        self.chips = 2 ** (len(self.gate_bits) - 1)

    def chip(self, index):
        return sum((index >> b & 1) << j for j, b in enumerate(self.gate_bits[1:]))

    def ring_position(self, chip):
        line, turn = chip >> 1, chip & 1
        return self.chips - 1 - line if turn else line

    def chip_at(self, position):
        position %= self.chips
        if position < self.chips // 2:
            return position << 1
        return (self.chips - 1 - position) << 1 | 1

    def shifted(self, index, step):
        chip = self.chip_at(self.ring_position(self.chip(index)) + step)
        for j, b in enumerate(self.gate_bits[1:]):
            index = index & ~(1 << b) | (chip >> j & 1) << b
        return index

    def ring(self, step):
        return [(i, self.shifted(i, step)) for i in range(self.size)]

    def flip(self, bit):
        return [(i, i ^ 1 << bit) for i in range(self.size)]

    def place_of(self, index):
        position = self.ring_position_traced(self.chip(index))
        half = self.chips // 2
        steps = [0] + [s for k in range(1, half) for s in (-k, k)] + [half]
        return index >> self.gate_bits[0] & 1, [self.chip_at_traced(position + s) for s in steps]

    def ring_position_traced(self, chip):
        line, turn = chip >> 1, chip & 1
        return jnp.where(turn == 1, self.chips - 1 - line, line)

    def chip_at_traced(self, position):
        position = position & self.chips - 1
        return jnp.where(position < self.chips // 2, position << 1, (self.chips - 1 - position) << 1 | 1)


STEPS = (1, -1)


def gather_ring(home, layout):
    blocks, ends = [home], [home, home]
    for _ in range(1, layout.chips // 2):
        ends = [lax.ppermute(end, "long", layout.ring(step)) for end, step in zip(ends, STEPS)]
        blocks += ends
    return blocks, [ends[0][:1], ends[1][1:]]


def last_step(tail, layout):
    return [lax.ppermute(end, "long", layout.ring(step)) for end, step in zip(tail, STEPS)]


def split(x):
    high = x.astype(BF16)
    return high, (x - high.astype(F32)).astype(BF16)


def dot(a, b, dims):
    return lax.dot_general(a, b, dims, preferred_element_type=F32)


def dot3(a, b, dims):
    return dot(a[0], b[0], dims) + (dot(a[0], b[1], dims) + dot(a[1], b[0], dims))


def turned(a):
    n = a.shape[1] // 2
    return jnp.concatenate([-a[:, n:], a[:, :n]], 1)


def as_matrix(a):
    n = a.shape[1] // 2
    return jnp.concatenate([jnp.concatenate([a[:, :n], -a[:, n:]], 1), jnp.concatenate([a[:, n:], a[:, :n]], 1)], 0)


def polar(e, beside=lambda gap: None):
    scale = lax.rsqrt(jnp.sum(e * e) + 1e-6)
    x = e
    n = x.shape[0]
    for k in range(NS_ITERS):
        xs = split(x)
        turns = [turned(v) for v in xs]
        beside(2 * k)
        h = jnp.concatenate([dot3(xs, xs, NT), dot3(xs, turns, NT)], 1)
        h = split(h * (scale * scale) if k == 0 else h)
        beside(2 * k + 1)
        rows = [jnp.concatenate(pair, 0) for pair in zip(xs, turns)]
        both = dot(jnp.concatenate(h, 0), rows[0], NN)
        x = 1.5 * x - 0.5 * (both[:n] + both[n:] + dot(h[0], rows[1], NN))
        x = x * scale if k == 0 else x
    return x


def load_pair(ref, pair):
    return [jnp.concatenate([ref[k, d, plane] for plane in range(2) for d in pair], 0) for k in range(2)]


def store_pair(ref, pair, y):
    n = y.shape[0] // 4
    for k, v in enumerate(split(y)):
        for plane in range(2):
            for t, d in enumerate(pair):
                ref[k, d, plane] = v[(2 * plane + t) * n : (2 * plane + t + 1) * n]


def apply_at(gate, source, target, pair):
    store_pair(target, pair, dot3(gate, load_pair(source, pair), NN))


def folded(total):
    n = total.shape[0] // 2
    return jnp.concatenate([total[:n, :n] + total[n:, n:], total[n:, :n] - total[:n, n:]], 1)


def environment(phi, psi, pairs):
    terms = [dot3(load_pair(phi, pair), load_pair(psi, pair), NT) for pair in pairs]
    return sum(terms[1:], terms[0])


def gate_matrix(gates_ref, section):
    return split(as_matrix(jnp.concatenate([gates_ref[section, 0], gates_ref[section, 1]], 1)))


def place(block, target, d):
    target[0, d], target[1, d] = split(block)


def joined(ref, d):
    return ref[0, d].astype(F32) + ref[1, d].astype(F32)


def unpacked(core, own, other):
    return jnp.concatenate([jnp.where(core == 0, own, other), jnp.where(core == 0, other, own)], 0).T


def pack_kernel(layout, x_ref, own_ref, sent_ref):
    core, _ = layout.place_of(lax.axis_index("long"))
    n = x_ref.shape[2] // 2
    for plane in range(2):
        t = x_ref[plane].T
        low, high = t[:n], t[n:]
        own_ref[plane] = jnp.where(core == 0, low, high)
        sent_ref[plane] = jnp.where(core == 0, high, low)


TURN = 1


def all_pairs(layout, bit):
    return [(d, d + (1 << bit)) for d in range(2 * layout.chips) if not d >> bit & 1]


def line_pairs(layout, bit, turn):
    return [tuple(d + (turn << TURN) for d in pair) for pair in all_pairs(layout, bit) if not pair[0] >> TURN & 1]


def chip_pairs(bit, chip):
    firsts = [(chip * 2 + slot) & ~(1 << bit) for slot in range(2)]
    return [(d, d + (1 << bit)) for d in firsts]


def near_pairs(layout, far):
    bit = layout.local_bits[0]
    others = [far ^ k for k in range(1, layout.chips) if not k >> bit - 1 & 1]
    return [pair for chip in others for pair in chip_pairs(bit, chip)]


def place_blocks(blocks, chips, core, target):
    for block, chip in zip(blocks, chips):
        for slot in range(2):
            place(block[slot], target, chip * 2 + (slot ^ core))


def place_far(halves, chip, core, target):
    for slot in range(2):
        place(halves[slot][0], target, chip * 2 + (slot ^ core))


def first_gate_kernel(layout, gates_ref, *refs):
    *blocks, phi_ref = refs
    core, chips = layout.place_of(lax.axis_index("long"))
    place_blocks(blocks, chips, core, phi_ref)
    gate = gate_matrix(gates_ref, 0)
    for pair in near_pairs(layout, chips[-1]):
        apply_at(gate, phi_ref, phi_ref, pair)


def line_kernel(layout, gates_ref, phi0_ref, phi1_ref, phi2_ref):
    _, chips = layout.place_of(lax.axis_index("long"))
    for s, source, target in ((1, phi0_ref, phi1_ref), (2, phi1_ref, phi2_ref)):
        gate = gate_matrix(gates_ref, s)
        for pair in line_pairs(layout, layout.local_bits[s], chips[0] & 1):
            apply_at(gate, source, target, pair)


def near_kernel(layout, *refs):
    *blocks, phi_ref, psi_ref, total_ref = refs
    core, chips = layout.place_of(lax.axis_index("long"))
    place_blocks(blocks, chips, core, psi_ref)
    total_ref[...] = environment(phi_ref, psi_ref, near_pairs(layout, chips[-1]))


def other_line_kernel(layout, gates_ref, far_a, far_b, phi0_in, phi1_in, phi2_in, phi0_ref, phi1_ref, phi2_ref):
    core, chips = layout.place_of(lax.axis_index("long"))
    place_far((far_a, far_b), chips[-1], core, phi0_ref)
    gate = gate_matrix(gates_ref, 0)
    for pair in chip_pairs(layout.local_bits[0], chips[-1]):
        apply_at(gate, phi0_ref, phi0_ref, pair)
    for s, source, target in ((1, phi0_ref, phi1_ref), (2, phi1_ref, phi2_ref)):
        gate = gate_matrix(gates_ref, s)
        for pair in line_pairs(layout, layout.local_bits[s], 1 - (chips[0] & 1)):
            apply_at(gate, source, target, pair)


def far_kernel(layout, psi_a, psi_b, total_ref, phi_ref, psi_in, psi_ref, e_ref):
    core, chips = layout.place_of(lax.axis_index("long"))
    far = chips[-1]
    place_far((psi_a, psi_b), far, core, psi_ref)
    e_ref[...] = folded(total_ref[...] + environment(phi_ref, psi_ref, chip_pairs(layout.local_bits[0], far)))


def last_adjoint_kernel(layout, gates_ref, phi_ref, next_ref, own_ref, sent_ref):
    core, chips = layout.place_of(lax.axis_index("long"))
    gate = gate_matrix(gates_ref, SECTIONS - 1)
    for pair in all_pairs(layout, layout.local_bits[SECTIONS - 1]):
        apply_at(gate, phi_ref, next_ref, pair)
    for slot, out in enumerate((own_ref, sent_ref)):
        out[...] = joined(next_ref, chips[0] * 2 + (slot ^ core))


def last_pair(layout, d):
    bit = layout.local_bits[SECTIONS - 1]
    first = d & ~(1 << bit)
    return first, first + (1 << bit)


def insert_bits(rest, bits):
    for bit in sorted(bits):
        rest = (rest >> bit << bit + 1) + (rest & (1 << bit) - 1)
    return rest


def load_quad(ref, rest, bits, plane):
    d = insert_bits(rest, bits)
    quad = [d + (t1 << bits[0]) + (t0 << bits[1]) for t1 in range(2) for t0 in range(2)]
    return [jnp.concatenate([ref[k, q, plane] for q in quad], 0) for k in range(2)]


def section_kernel(layout, section, e0_ref, e1_ref, phi_ref, psi_ref, gate_ref, e_ref, joint, left):
    bits = layout.local_bits[section + 1], layout.local_bits[section]
    rests = psi_ref.shape[1] // 4
    q = joint.shape[0] // 2
    c = q // 4
    units = [(rest, u) for rest in range(rests) for u in range(2)]
    gaps = 2 * NS_ITERS - 2

    def add(rest, u):
        planes = [load_quad(phi_ref, rest, bits, p) for p in range(2)]
        term = dot3([jnp.concatenate(v, 0) for v in zip(*planes)], load_quad(psi_ref, rest, bits, u), NT)
        at = (slice(None), slice(u * q, u * q + q))
        joint[at] = term if rest == 0 else joint[at] + term

    def arrange(p):
        real = joint[:q, :q] + joint[q:, q:] if p == 0 else joint[q:, :q] - joint[:q, q:]
        for k, v in enumerate(split(real)):
            for u1 in range(2):
                for t1 in range(2):
                    for t0 in range(2):
                        rows = slice((u1 * 2 + t1) * c, (u1 * 2 + t1 + 1) * c)
                        lanes = slice((p * 2 + t0) * 2 * c, (p * 2 + t0 + 1) * 2 * c)
                        left[k, rows, lanes] = v[(t1 * 2 + t0) * c : (t1 * 2 + t0 + 1) * c, u1 * 2 * c : (u1 + 1) * 2 * c]

    def beside(gap):
        for unit in units[gap * len(units) // gaps : (gap + 1) * len(units) // gaps] if gap < gaps else ():
            add(*unit)
        if gap >= gaps:
            arrange(gap - gaps)

    x = polar(e0_ref[...] + e1_ref[...], beside)
    right = []
    for v in split(x):
        r0, r1, i0, i1 = v[:c, : 2 * c], v[c:, : 2 * c], v[:c, 2 * c :], v[c:, 2 * c :]
        right.append(
            jnp.concatenate([jnp.concatenate([r0, r1, i0, i1], 1), jnp.concatenate([-i0, -i1, r0, r1], 1)], 0)
        )
    two = dot(left[0], jnp.concatenate(right, 0), NT)
    out = two[:, : 2 * c] + two[:, 2 * c :] + dot(left[1], right[0], NT)
    first, second = out[: 2 * c], out[2 * c :]
    e_ref[...] = jnp.concatenate([first[:, :c], second[:, :c], first[:, c:], second[:, c:]], 1)
    gate_ref[0], gate_ref[1] = split(as_matrix(x))


def apply_kernel(layout, section, gate_ref, psi_ref, next_ref):
    gate = gate_ref[0], gate_ref[1]
    for pair in all_pairs(layout, layout.local_bits[section]):
        apply_at(gate, psi_ref, next_ref, pair)


def ends_kernel(layout, gate_ref, psi_ref, own_ref, sent_ref):
    core, chips = layout.place_of(lax.axis_index("long"))
    gate = gate_ref[0], gate_ref[1]
    n = own_ref.shape[2]
    for t, first in enumerate(last_pair(layout, chips[0] * 2)):
        y = dot3(gate, load_pair(psi_ref, (first, first + 1)), NN)
        for plane in range(2):
            low, high = y[2 * plane * n : (2 * plane + 1) * n], y[(2 * plane + 1) * n : (2 * plane + 2) * n]
            own_ref[t, plane] = jnp.where(core == 0, low, high)
            sent_ref[t, plane] = jnp.where(core == 0, high, low)


def last_polar_kernel(e0_ref, e1_ref, adjoint_ref, gate_ref, out_ref, sem):
    copy = pltpu.make_async_copy(adjoint_ref, out_ref, sem)
    copy.start()
    gate_ref[...] = as_matrix(polar(e0_ref[...] + e1_ref[...]))
    copy.wait()


def unpack_kernel(layout, own_ref, got_ref, out_ref):
    core, _ = layout.place_of(lax.axis_index("long"))
    for plane in range(2):
        out_ref[plane] = unpacked(core, own_ref[plane], got_ref[plane])


def last_apply_kernel(layout, gate_ref, psi_own, psi_got, out_ref, state, sems):
    core, chips = layout.place_of(lax.axis_index("long"))
    t = chips[0] * 2 + core >> layout.local_bits[SECTIONS - 1] & 1
    n = psi_own.shape[2]
    gate = split(jnp.concatenate([gate_ref[pl.ds(pl.multiple_of((plane * 2 + t) * n, n), n)] for plane in range(2)], 0))
    halves = [
        dot3(gate, split(jnp.concatenate([psi[0, 0], psi[1, 0], psi[0, 1], psi[1, 1]], 0)), NN)
        for psi in (psi_own, psi_got)
    ]
    copies = []
    for plane in range(2):
        state[plane] = unpacked(core, *[y[plane * n : (plane + 1) * n] for y in halves])
        copies.append(pltpu.make_async_copy(state.at[plane], out_ref.at[plane], sems.at[plane]))
        copies[plane].start()
    for copy in copies:
        copy.wait()


def call(kernel, name, outs, ins, flops, scratch=(), aliases=None, out_spaces={}):
    sizes = [int(np.prod(a.shape)) * a.dtype.itemsize for a in list(ins) + list(outs)]
    spec = pl.BlockSpec(memory_space=pltpu.VMEM)
    return pl.pallas_call(
        kernel,
        out_shape=outs,
        in_specs=[spec] * len(ins),
        out_specs=[pl.BlockSpec(memory_space=out_spaces.get(k, pltpu.VMEM)) for k in range(len(outs))],
        scratch_shapes=list(scratch),
        input_output_aliases=aliases or {},
        compiler_params=pltpu.CompilerParams(vmem_limit_bytes=VMEM_LIMIT),
        cost_estimate=pl.CostEstimate(flops=flops, bytes_accessed=sum(sizes), transcendentals=0),
        name=name,
    )(*ins)


def shards(initial_state, adjoint_state, current_gates):
    layout = Layout(lax.axis_size("long"))
    core_flip = layout.flip(layout.gate_bits[0])
    rows, lanes = initial_state.shape[1:]
    c = lanes // 2
    devices = layout.chips * 2
    whole = jax.ShapeDtypeStruct(initial_state.shape, F32)
    slab = jax.ShapeDtypeStruct((2, c, rows), F32)
    two_slabs = jax.ShapeDtypeStruct((2, 2, c, rows), F32)
    pieces = jax.ShapeDtypeStruct((2, devices, 2, c, rows), BF16)
    env = jax.ShapeDtypeStruct((lanes, 2 * lanes), F32)
    square = jax.ShapeDtypeStruct((2 * lanes, 2 * lanes), F32)
    apply_flops = 3 * 2 * (2 * lanes) ** 2 * (devices // 2) * rows

    def kernel(body, *args):
        return functools.partial(body, layout, *args)

    def both(e):
        for bit in layout.other_bits:
            e = e + lax.ppermute(e, "long", layout.flip(bit))
        return e, lax.ppermute(e, "long", core_flip)

    def home(own, sent):
        return jnp.stack([own, lax.ppermute(sent, "long", core_flip)])

    def pack(state):
        return call(kernel(pack_kernel), "pack", [slab] * 2, [state], 0)

    def after(x, *others):
        return lax.optimization_barrier((x, *others))[0]

    phi_home = home(*pack(adjoint_state))
    psi_own, psi_sent = pack(initial_state)
    psi_sent = after(psi_sent, phi_home)
    phi_near, phi_tail = gather_ring(phi_home, layout)
    phis = [call(kernel(first_gate_kernel), "first_gate", [pieces], [current_gates] + phi_near, apply_flops)[0]]
    phi_far = last_step(phi_tail, layout)
    phis += call(kernel(line_kernel), "line", [pieces] * 2, [current_gates, phis[0]], apply_flops)
    psi_near, psi_tail = gather_ring(home(psi_own, psi_sent), layout)
    psi_far = last_step([psi_tail[0], after(psi_tail[1], phis[1])], layout)
    psi, total = call(kernel(near_kernel), "near", [pieces, square], psi_near + [phis[0]], 3 * apply_flops // 4)
    phis = list(
        call(
            kernel(other_line_kernel),
            "other_line",
            [pieces] * 3,
            [current_gates] + phi_far + phis,
            5 * apply_flops // 4,
            aliases={3: 0, 4: 1, 5: 2},
        )
    )
    total = after(total, phis[2])
    psi, e = call(
        kernel(far_kernel), "far", [pieces, env], psi_far + [total, phis[0], psi], apply_flops // 4, aliases={4: 0}
    )
    gate_pair = jax.ShapeDtypeStruct((2,) + square.shape, BF16)
    for section in range(SECTIONS - 1):
        e0, e1 = both(e)
        if section == 0:
            phi, phi_own, phi_sent = call(
                kernel(last_adjoint_kernel),
                "last_adjoint",
                [pieces, slab, slab],
                [current_gates, phis[2]],
                apply_flops,
            )
            phis.append(phi)
            psi = after(psi, phi)
        else:
            (psi,) = call(kernel(apply_kernel, section - 1), "apply", [pieces], [gate, psi], apply_flops)
        if section == 1:
            phi_got = lax.ppermute(after(phi_sent, e), "long", core_flip)
        gate, e = call(
            kernel(section_kernel, section),
            "section",
            [gate_pair, env],
            [e0, e1, phis[section + 1], psi],
            4 * apply_flops,
            [pltpu.VMEM((4 * lanes, 4 * lanes), F32), pltpu.VMEM((2, 2 * lanes, 4 * lanes), BF16)],
        )
    e0, e1 = both(e)
    psi_own, psi_sent = call(kernel(ends_kernel), "ends", [two_slabs, two_slabs], [gate, psi], apply_flops // 4)
    psi_got = lax.ppermute(psi_sent, "long", core_flip)
    (adjoint,) = call(kernel(unpack_kernel), "unpack", [whole], [after(phi_own, e), phi_got], 0)
    gate, final_adjoint = call(
        last_polar_kernel,
        "last_polar",
        [square, whole],
        [e0, e1, adjoint],
        2 * apply_flops,
        [pltpu.SemaphoreType.DMA],
        out_spaces={1: pl.ANY},
    )
    (final_state,) = call(
        kernel(last_apply_kernel),
        "last_apply",
        [whole],
        [gate, psi_own, psi_got],
        apply_flops // 4,
        [pltpu.VMEM(initial_state.shape, F32), pltpu.SemaphoreType.DMA((2,))],
        out_spaces={0: pl.ANY},
    )
    return final_state, final_adjoint


def solution(mesh):
    return jax.shard_map(
        shards,
        mesh=mesh,
        in_specs=(
            P(None, ("groups", "long"), None),
            P(None, ("groups", "long"), None),
            P("groups", None, None, None),
        ),
        out_specs=(P(None, ("groups", "long"), None), P(None, ("groups", "long"), None)),
        check_vma=False,
    )
```

```python
import functools

import jax
import jax.numpy as jnp
import numpy as np
from jax import lax
from jax.experimental import pallas as pl
from jax.experimental.pallas import tpu as pltpu
from jax.sharding import PartitionSpec as P

SECTIONS = 4
NS_ITERS = 8

F32, BF16 = jnp.float32, jnp.bfloat16
NN = (((1,), (0,)), ((), ()))
NT = (((1,), (1,)), ((), ()))
VMEM_LIMIT = 24 * 2**20


class Layout:
    def __init__(self, size):
        bits = size.bit_length() - 1
        self.size = size
        self.partner_bits = [bits - 1, bits // 2, 0, 1]
        self.gate_bits = sorted(set(self.partner_bits))
        self.other_bits = [b for b in range(bits) if b not in self.gate_bits]
        self.local_bits = [self.gate_bits.index(b) for b in self.partner_bits]
        self.chips = 2 ** (len(self.gate_bits) - 1)

    def chip(self, index):
        return sum((index >> b & 1) << j for j, b in enumerate(self.gate_bits[1:]))

    def ring_position(self, chip):
        line, turn = chip >> 1, chip & 1
        return self.chips - 1 - line if turn else line

    def chip_at(self, position):
        position %= self.chips
        if position < self.chips // 2:
            return position << 1
        return (self.chips - 1 - position) << 1 | 1

    def shifted(self, index, step):
        chip = self.chip_at(self.ring_position(self.chip(index)) + step)
        for j, b in enumerate(self.gate_bits[1:]):
            index = index & ~(1 << b) | (chip >> j & 1) << b
        return index

    def ring(self, step):
        return [(i, self.shifted(i, step)) for i in range(self.size)]

    def flip(self, bit):
        return [(i, i ^ 1 << bit) for i in range(self.size)]

    def place_of(self, index):
        position = self.ring_position_traced(self.chip(index))
        half = self.chips // 2
        steps = [0] + [s for k in range(1, half) for s in (-k, k)] + [half]
        return index >> self.gate_bits[0] & 1, [self.chip_at_traced(position + s) for s in steps]

    def ring_position_traced(self, chip):
        line, turn = chip >> 1, chip & 1
        return jnp.where(turn == 1, self.chips - 1 - line, line)

    def chip_at_traced(self, position):
        position = position & self.chips - 1
        return jnp.where(position < self.chips // 2, position << 1, (self.chips - 1 - position) << 1 | 1)


STEPS = (1, -1)


def gather_ring(home, layout):
    blocks, ends = [home], [home, home]
    for _ in range(1, layout.chips // 2):
        ends = [lax.ppermute(end, "long", layout.ring(step)) for end, step in zip(ends, STEPS)]
        blocks += ends
    return blocks, [ends[0][:1], ends[1][1:]]


def last_step(tail, layout):
    return [lax.ppermute(end, "long", layout.ring(step)) for end, step in zip(tail, STEPS)]


def split(x):
    high = x.astype(BF16)
    return high, (x - high.astype(F32)).astype(BF16)


def dot(a, b, dims):
    return lax.dot_general(a, b, dims, preferred_element_type=F32)


def dot3(a, b, dims):
    return dot(a[0], b[0], dims) + (dot(a[0], b[1], dims) + dot(a[1], b[0], dims))


def turned(a):
    n = a.shape[1] // 2
    return jnp.concatenate([-a[:, n:], a[:, :n]], 1)


def as_matrix(a):
    n = a.shape[1] // 2
    return jnp.concatenate([jnp.concatenate([a[:, :n], -a[:, n:]], 1), jnp.concatenate([a[:, n:], a[:, :n]], 1)], 0)


def polar(e, beside=lambda gap: None):
    scale = lax.rsqrt(jnp.sum(e * e) + 1e-6)
    x = e
    n = x.shape[0]
    for k in range(NS_ITERS):
        xs = split(x)
        turns = [turned(v) for v in xs]
        beside(2 * k)
        h = jnp.concatenate([dot3(xs, xs, NT), dot3(xs, turns, NT)], 1)
        h = split(h * (-0.5 * scale * scale) if k == 0 else -0.5 * h)
        beside(2 * k + 1)
        rows = [jnp.concatenate(pair, 0) for pair in zip(xs, turns)]
        both = dot(jnp.concatenate(h, 0), rows[0], NN)
        x = 1.5 * x + (both[:n] + both[n:] + dot(h[0], rows[1], NN))
        x = x * scale if k == 0 else x
    return x


def load_pair(ref, pair):
    return [jnp.concatenate([ref[k, d, plane] for plane in range(2) for d in pair], 0) for k in range(2)]


def store_pair(ref, pair, y):
    n = y.shape[0] // 4
    for k, v in enumerate(split(y)):
        for plane in range(2):
            for t, d in enumerate(pair):
                ref[k, d, plane] = v[(2 * plane + t) * n : (2 * plane + t + 1) * n]


def apply_at(gate, source, target, pair):
    store_pair(target, pair, dot3(gate, load_pair(source, pair), NN))


def folded(total):
    n = total.shape[0] // 2
    return jnp.concatenate([total[:n, :n] + total[n:, n:], total[n:, :n] - total[:n, n:]], 1)


def environment(phi, psi, pairs):
    terms = [dot3(load_pair(phi, pair), load_pair(psi, pair), NT) for pair in pairs]
    return sum(terms[1:], terms[0])


def gate_matrix(gates_ref, section):
    return split(as_matrix(jnp.concatenate([gates_ref[section, 0], gates_ref[section, 1]], 1)))


def place(block, target, d):
    target[0, d], target[1, d] = split(block)


def joined(ref, d):
    return ref[0, d].astype(F32) + ref[1, d].astype(F32)


def unpacked(core, own, other):
    return jnp.concatenate([jnp.where(core == 0, own, other), jnp.where(core == 0, other, own)], 0).T


def pack_kernel(layout, x_ref, own_ref, sent_ref):
    core, _ = layout.place_of(lax.axis_index("long"))
    n = x_ref.shape[2] // 2
    for plane in range(2):
        t = x_ref[plane].T
        low, high = t[:n], t[n:]
        own_ref[plane] = jnp.where(core == 0, low, high)
        sent_ref[plane] = jnp.where(core == 0, high, low)


TURN = 1


def all_pairs(layout, bit):
    return [(d, d + (1 << bit)) for d in range(2 * layout.chips) if not d >> bit & 1]


def line_pairs(layout, bit, turn):
    return [tuple(d + (turn << TURN) for d in pair) for pair in all_pairs(layout, bit) if not pair[0] >> TURN & 1]


def chip_pairs(bit, chip):
    firsts = [(chip * 2 + slot) & ~(1 << bit) for slot in range(2)]
    return [(d, d + (1 << bit)) for d in firsts]


def near_pairs(layout, far):
    bit = layout.local_bits[0]
    others = [far ^ k for k in range(1, layout.chips) if not k >> bit - 1 & 1]
    return [pair for chip in others for pair in chip_pairs(bit, chip)]


def place_blocks(blocks, chips, core, target):
    for block, chip in zip(blocks, chips):
        for slot in range(2):
            place(block[slot], target, chip * 2 + (slot ^ core))


def place_far(halves, chip, core, target):
    for slot in range(2):
        place(halves[slot][0], target, chip * 2 + (slot ^ core))


def first_gate_kernel(layout, gates_ref, *refs):
    *blocks, phi_ref = refs
    core, chips = layout.place_of(lax.axis_index("long"))
    place_blocks(blocks, chips, core, phi_ref)
    gate = gate_matrix(gates_ref, 0)
    for pair in near_pairs(layout, chips[-1]):
        apply_at(gate, phi_ref, phi_ref, pair)


def line_kernel(layout, gates_ref, phi0_ref, phi1_ref, phi2_ref):
    _, chips = layout.place_of(lax.axis_index("long"))
    for s, source, target in ((1, phi0_ref, phi1_ref), (2, phi1_ref, phi2_ref)):
        gate = gate_matrix(gates_ref, s)
        for pair in line_pairs(layout, layout.local_bits[s], chips[0] & 1):
            apply_at(gate, source, target, pair)


def near_kernel(layout, *refs):
    *blocks, phi_ref, psi_ref, total_ref = refs
    core, chips = layout.place_of(lax.axis_index("long"))
    place_blocks(blocks, chips, core, psi_ref)
    total_ref[...] = environment(phi_ref, psi_ref, near_pairs(layout, chips[-1]))


def other_line_kernel(layout, gates_ref, far_a, far_b, phi0_in, phi1_in, phi2_in, phi0_ref, phi1_ref, phi2_ref):
    core, chips = layout.place_of(lax.axis_index("long"))
    place_far((far_a, far_b), chips[-1], core, phi0_ref)
    gate = gate_matrix(gates_ref, 0)
    for pair in chip_pairs(layout.local_bits[0], chips[-1]):
        apply_at(gate, phi0_ref, phi0_ref, pair)
    for s, source, target in ((1, phi0_ref, phi1_ref), (2, phi1_ref, phi2_ref)):
        gate = gate_matrix(gates_ref, s)
        for pair in line_pairs(layout, layout.local_bits[s], 1 - (chips[0] & 1)):
            apply_at(gate, source, target, pair)


def far_kernel(layout, psi_a, psi_b, total_ref, phi_ref, psi_in, psi_ref, e_ref):
    core, chips = layout.place_of(lax.axis_index("long"))
    far = chips[-1]
    place_far((psi_a, psi_b), far, core, psi_ref)
    e_ref[...] = folded(total_ref[...] + environment(phi_ref, psi_ref, chip_pairs(layout.local_bits[0], far)))


def last_adjoint_kernel(layout, gates_ref, phi_ref, next_ref, own_ref, sent_ref):
    core, chips = layout.place_of(lax.axis_index("long"))
    gate = gate_matrix(gates_ref, SECTIONS - 1)
    for pair in all_pairs(layout, layout.local_bits[SECTIONS - 1]):
        apply_at(gate, phi_ref, next_ref, pair)
    for slot, out in enumerate((own_ref, sent_ref)):
        out[...] = joined(next_ref, chips[0] * 2 + (slot ^ core))


def last_pair(layout, d):
    bit = layout.local_bits[SECTIONS - 1]
    first = d & ~(1 << bit)
    return first, first + (1 << bit)


def insert_bits(rest, bits):
    for bit in sorted(bits):
        rest = (rest >> bit << bit + 1) + (rest & (1 << bit) - 1)
    return rest


def load_quad(ref, rest, bits, plane):
    d = insert_bits(rest, bits)
    quad = [d + (t1 << bits[0]) + (t0 << bits[1]) for t1 in range(2) for t0 in range(2)]
    return [jnp.concatenate([ref[k, q, plane] for q in quad], 0) for k in range(2)]


def section_kernel(layout, section, e0_ref, e1_ref, phi_ref, psi_ref, gate_ref, e_ref, joint, left):
    bits = layout.local_bits[section + 1], layout.local_bits[section]
    rests = psi_ref.shape[1] // 4
    q = joint.shape[0] // 2
    c = q // 4
    units = [(rest, u) for rest in range(rests) for u in range(2)]
    gaps = 2 * NS_ITERS - 2

    def add(rest, u):
        planes = [load_quad(phi_ref, rest, bits, p) for p in range(2)]
        term = dot3([jnp.concatenate(v, 0) for v in zip(*planes)], load_quad(psi_ref, rest, bits, u), NT)
        at = (slice(None), slice(u * q, u * q + q))
        joint[at] = term if rest == 0 else joint[at] + term

    def arrange(p):
        real = joint[:q, :q] + joint[q:, q:] if p == 0 else joint[q:, :q] - joint[:q, q:]
        for k, v in enumerate(split(real)):
            for u1 in range(2):
                for t1 in range(2):
                    for t0 in range(2):
                        rows = slice((u1 * 2 + t1) * c, (u1 * 2 + t1 + 1) * c)
                        lanes = slice((p * 2 + t0) * 2 * c, (p * 2 + t0 + 1) * 2 * c)
                        left[k, rows, lanes] = v[(t1 * 2 + t0) * c : (t1 * 2 + t0 + 1) * c, u1 * 2 * c : (u1 + 1) * 2 * c]

    def beside(gap):
        for unit in units[gap * len(units) // gaps : (gap + 1) * len(units) // gaps] if gap < gaps else ():
            add(*unit)
        if gap >= gaps:
            arrange(gap - gaps)

    x = polar(e0_ref[...] + e1_ref[...], beside)
    right = []
    for v in split(x):
        r0, r1, i0, i1 = v[:c, : 2 * c], v[c:, : 2 * c], v[:c, 2 * c :], v[c:, 2 * c :]
        right.append(
            jnp.concatenate([jnp.concatenate([r0, r1, i0, i1], 1), jnp.concatenate([-i0, -i1, r0, r1], 1)], 0)
        )
    two = dot(left[0], jnp.concatenate(right, 0), NT)
    out = two[:, : 2 * c] + two[:, 2 * c :] + dot(left[1], right[0], NT)
    first, second = out[: 2 * c], out[2 * c :]
    e_ref[...] = jnp.concatenate([first[:, :c], second[:, :c], first[:, c:], second[:, c:]], 1)
    gate_ref[0], gate_ref[1] = split(as_matrix(x))


def apply_kernel(layout, section, gate_ref, psi_ref, next_ref):
    gate = gate_ref[0], gate_ref[1]
    for pair in all_pairs(layout, layout.local_bits[section]):
        apply_at(gate, psi_ref, next_ref, pair)


def ends_kernel(layout, gate_ref, psi_ref, own_ref, sent_ref):
    core, chips = layout.place_of(lax.axis_index("long"))
    gate = gate_ref[0], gate_ref[1]
    n = own_ref.shape[2]
    for t, first in enumerate(last_pair(layout, chips[0] * 2)):
        y = dot3(gate, load_pair(psi_ref, (first, first + 1)), NN)
        for plane in range(2):
            low, high = y[2 * plane * n : (2 * plane + 1) * n], y[(2 * plane + 1) * n : (2 * plane + 2) * n]
            own_ref[t, plane] = jnp.where(core == 0, low, high)
            sent_ref[t, plane] = jnp.where(core == 0, high, low)


def last_polar_kernel(e0_ref, e1_ref, adjoint_ref, gate_ref, out_ref, sem):
    copy = pltpu.make_async_copy(adjoint_ref, out_ref, sem)
    copy.start()
    gate_ref[...] = as_matrix(polar(e0_ref[...] + e1_ref[...]))
    copy.wait()


def unpack_kernel(layout, own_ref, got_ref, out_ref):
    core, _ = layout.place_of(lax.axis_index("long"))
    for plane in range(2):
        out_ref[plane] = unpacked(core, own_ref[plane], got_ref[plane])


def last_apply_kernel(layout, gate_ref, psi_own, psi_got, out_ref, state, sems):
    core, chips = layout.place_of(lax.axis_index("long"))
    t = chips[0] * 2 + core >> layout.local_bits[SECTIONS - 1] & 1
    n = psi_own.shape[2]
    gate = split(jnp.concatenate([gate_ref[pl.ds(pl.multiple_of((plane * 2 + t) * n, n), n)] for plane in range(2)], 0))
    halves = [
        dot3(gate, split(jnp.concatenate([psi[0, 0], psi[1, 0], psi[0, 1], psi[1, 1]], 0)), NN)
        for psi in (psi_own, psi_got)
    ]
    copies = []
    for plane in range(2):
        state[plane] = unpacked(core, *[y[plane * n : (plane + 1) * n] for y in halves])
        copies.append(pltpu.make_async_copy(state.at[plane], out_ref.at[plane], sems.at[plane]))
        copies[plane].start()
    for copy in copies:
        copy.wait()


def call(kernel, name, outs, ins, flops, scratch=(), aliases=None, out_spaces={}):
    sizes = [int(np.prod(a.shape)) * a.dtype.itemsize for a in list(ins) + list(outs)]
    spec = pl.BlockSpec(memory_space=pltpu.VMEM)
    return pl.pallas_call(
        kernel,
        out_shape=outs,
        in_specs=[spec] * len(ins),
        out_specs=[pl.BlockSpec(memory_space=out_spaces.get(k, pltpu.VMEM)) for k in range(len(outs))],
        scratch_shapes=list(scratch),
        input_output_aliases=aliases or {},
        compiler_params=pltpu.CompilerParams(vmem_limit_bytes=VMEM_LIMIT),
        cost_estimate=pl.CostEstimate(flops=flops, bytes_accessed=sum(sizes), transcendentals=0),
        name=name,
    )(*ins)


def shards(initial_state, adjoint_state, current_gates):
    layout = Layout(lax.axis_size("long"))
    core_flip = layout.flip(layout.gate_bits[0])
    rows, lanes = initial_state.shape[1:]
    c = lanes // 2
    devices = layout.chips * 2
    whole = jax.ShapeDtypeStruct(initial_state.shape, F32)
    slab = jax.ShapeDtypeStruct((2, c, rows), F32)
    two_slabs = jax.ShapeDtypeStruct((2, 2, c, rows), F32)
    pieces = jax.ShapeDtypeStruct((2, devices, 2, c, rows), BF16)
    env = jax.ShapeDtypeStruct((lanes, 2 * lanes), F32)
    square = jax.ShapeDtypeStruct((2 * lanes, 2 * lanes), F32)
    apply_flops = 3 * 2 * (2 * lanes) ** 2 * (devices // 2) * rows

    def kernel(body, *args):
        return functools.partial(body, layout, *args)

    def both(e):
        for bit in layout.other_bits:
            e = e + lax.ppermute(e, "long", layout.flip(bit))
        return e, lax.ppermute(e, "long", core_flip)

    def home(own, sent):
        return jnp.stack([own, lax.ppermute(sent, "long", core_flip)])

    def pack(state):
        return call(kernel(pack_kernel), "pack", [slab] * 2, [state], 0)

    def after(x, *others):
        return lax.optimization_barrier((x, *others))[0]

    phi_home = home(*pack(adjoint_state))
    psi_own, psi_sent = pack(initial_state)
    phi_home, psi_own, psi_sent = lax.optimization_barrier((phi_home, psi_own, psi_sent))
    phi_near, phi_tail = gather_ring(phi_home, layout)
    phis = [call(kernel(first_gate_kernel), "first_gate", [pieces], [current_gates] + phi_near, apply_flops)[0]]
    phi_far = last_step(phi_tail, layout)
    phis += call(kernel(line_kernel), "line", [pieces] * 2, [current_gates, phis[0]], apply_flops)
    psi_near, psi_tail = gather_ring(home(psi_own, psi_sent), layout)
    psi_far = last_step([psi_tail[0], after(psi_tail[1], phis[1])], layout)
    psi, total = call(kernel(near_kernel), "near", [pieces, square], psi_near + [phis[0]], 3 * apply_flops // 4)
    phis = list(
        call(
            kernel(other_line_kernel),
            "other_line",
            [pieces] * 3,
            [current_gates] + phi_far + phis,
            5 * apply_flops // 4,
            aliases={3: 0, 4: 1, 5: 2},
        )
    )
    total = after(total, phis[2])
    psi, e = call(
        kernel(far_kernel), "far", [pieces, env], psi_far + [total, phis[0], psi], apply_flops // 4, aliases={4: 0}
    )
    gate_pair = jax.ShapeDtypeStruct((2,) + square.shape, BF16)
    for section in range(SECTIONS - 1):
        e0, e1 = both(e)
        if section == 0:
            phi, phi_own, phi_sent = call(
                kernel(last_adjoint_kernel),
                "last_adjoint",
                [pieces, slab, slab],
                [current_gates, phis[2]],
                apply_flops,
            )
            phis.append(phi)
            psi = after(psi, phi)
        else:
            (psi,) = call(kernel(apply_kernel, section - 1), "apply", [pieces], [gate, psi], apply_flops)
        if section == 1:
            phi_got = lax.ppermute(after(phi_sent, e), "long", core_flip)
        gate, e = call(
            kernel(section_kernel, section),
            "section",
            [gate_pair, env],
            [e0, e1, phis[section + 1], psi],
            4 * apply_flops,
            [pltpu.VMEM((4 * lanes, 4 * lanes), F32), pltpu.VMEM((2, 2 * lanes, 4 * lanes), BF16)],
        )
    e0, e1 = both(e)
    psi_own, psi_sent = call(kernel(ends_kernel), "ends", [two_slabs, two_slabs], [gate, psi], apply_flops // 4)
    psi_got = lax.ppermute(psi_sent, "long", core_flip)
    (adjoint,) = call(kernel(unpack_kernel), "unpack", [whole], [after(phi_own, e), phi_got], 0)
    gate, final_adjoint = call(
        last_polar_kernel,
        "last_polar",
        [square, whole],
        [e0, e1, adjoint],
        2 * apply_flops,
        [pltpu.SemaphoreType.DMA],
        out_spaces={1: pl.ANY},
    )
    (final_state,) = call(
        kernel(last_apply_kernel),
        "last_apply",
        [whole],
        [gate, psi_own, psi_got],
        apply_flops // 4,
        [pltpu.VMEM(initial_state.shape, F32), pltpu.SemaphoreType.DMA((2,))],
        out_spaces={0: pl.ANY},
    )
    return final_state, final_adjoint


def solution(mesh):
    return jax.shard_map(
        shards,
        mesh=mesh,
        in_specs=(
            P(None, ("groups", "long"), None),
            P(None, ("groups", "long"), None),
            P("groups", None, None, None),
        ),
        out_specs=(P(None, ("groups", "long"), None), P(None, ("groups", "long"), None)),
        check_vma=False,
    )
```
